32 devices in a mesh: groups: 2 (over y), patch: 4 (over z), head: 4 (over x, core).
Axes of the slice: x: 2, y: 2, z: 4, core: 2. Of those that a mesh axis runs over, the one named last changes fastest.
Arguments:
- queries: bfloat16 [1024, 2560], P(('groups', 'patch', 'head')), parts along dimension 0, may hold values from -500 to 500
- keys: bfloat16 [1024, 2560], P(('groups', 'patch', 'head')), parts along dimension 0, may hold values from -500 to 500
- values: bfloat16 [1024, 2560], P(('groups', 'patch', 'head')), parts along dimension 0, may hold values from -6 to 6
- q_gain: float32 [2560], replicated, may hold values from 1.2 to 2
- k_gain: float32 [2560], replicated, may hold values from 1.2 to 2
- prev_keys: bfloat16 [1024, 2560], P('groups', 'head'), parts along dimension 0, may hold values from -200 to 200
- prev_values: bfloat16 [1024, 2560], P('groups', 'head'), parts along dimension 0, may hold values from -6 to 6
- res_keys: bfloat16 [16, 16, 2560], P(('groups', 'patch'), None, 'head'), parts along dimension 0, may hold values from -3 to 3
- res_values: bfloat16 [16, 16, 2560], P(('groups', 'patch'), None, 'head'), parts along dimension 0, may hold values from -3 to 3
- block_ids: int32 [16], P(('groups', 'patch')), parts along dimension 0, may hold values from 0 to 7, as said below
- scale_exps: int32 [16, 20], P(('groups', 'patch'), 'head'), parts along dimension 0, may hold values from -2 to 1
Outputs:
- attended: bfloat16 [1024, 2560], P(('groups', 'patch', 'head')), parts along dimension 0
The draws below stay inside these ranges and needn't reach their ends.
There are 2 independent parts, one for each index of `groups`. The reference program is written for one: setup_inputs(seed, part) draws one part's arguments, and reference() takes and returns one part's arrays. A program takes and returns all parts, laid end to end along the dimension named above; an argument that names none is the same for every part. Nothing has to cross between parts.
Inputs may be any that keep to these rules, and one draw needn't show every extreme that they name: `block_ids`: the 2 entries of one patch are distinct block numbers of that patch.
All inputs are finite; a program needn't handle non-finite values.
Results may differ from the reference program's by a relative error of at most 0.004.
The reference program's roundings to bfloat16 on the way (of `q_norm`, `k_norm`, `stale_keys`, `stale_values`, `key_set` and `weights`) count: a program that leaves them out, or rounds other values in their place, can miss the bound.
Values may be sent and summed in bfloat16 or wider, within the bound.
No kernel may reach another device: no remote copies, remote signals or barrier semaphores. Data moves between devices by JAX's collectives and lax.ppermute only.
A program may use at most 128 MiB of HBM per device.

```python
import math
import jax
import jax.numpy as jnp
from jax import lax

HEADS = 20
HEAD_DIM = 128
FEAT = 2560
TOK_PATCH = 128
NBLK = 8
SEND = 2
BLK = 16
TOKENS = 512
SENT = 8


def shared_draw(key):
    normal_part = jnp.clip(jax.random.normal(key, (TOKENS, HEADS * HEAD_DIM), jnp.float32), -5.0, 5.0)
    return normal_part


def draw_queries(key, part):
    normal_part = shared_draw(key)
    return normal_part.astype(jnp.bfloat16)


def draw_keys(key, part):
    key = jax.random.fold_in(key, 4)
    normal_part = jnp.clip(jax.random.normal(key, (TOKENS, HEADS * HEAD_DIM), jnp.float32), -5.0, 5.0)
    return normal_part.astype(jnp.bfloat16)


def draw_prev_keys(key, part):
    key = jax.random.fold_in(key, 5)
    stale_base = 1.6 * jnp.clip(jax.random.normal(key, (TOKENS, HEADS * HEAD_DIM), jnp.float32), -5.0, 5.0)
    return stale_base.astype(jnp.bfloat16)


def draw_block_ids(key, part):
    key = jax.random.fold_in(key, 6)
    patch_count = SENT // SEND
    ranking = jax.random.randint(key, (patch_count, NBLK), 0, 1 << 20) * NBLK + jnp.arange(NBLK, dtype=jnp.int32)[None, :]
    ranking = ranking.at[0, NBLK - 1].set(-1)
    ranking = ranking.at[1, 0].set(-1)
    chosen = jnp.argsort(ranking, axis=1, stable=True)[:, :SEND]
    return chosen.reshape(SENT).astype(jnp.int32)


def place_ends(values, stream_key, least, top_value):
    longest = values.shape.index(max(values.shape))
    spots = []
    for shift in (0, 1):
        where = [jax.random.randint(jax.random.fold_in(stream_key, axis), (), 0, length) for axis, length in enumerate(values.shape)]
        where[longest] = (where[longest] + shift) % values.shape[longest]
        spots.append(tuple(where))
    return values.at[spots[0]].set(least).at[spots[1]].set(top_value)


def level_of(stream_key, dims, split, low, largest):
    loudness, own = 1.0, jax.random.fold_in(stream_key, 6)
    for position, shards_of in split:
        steps = jnp.exp(jax.random.uniform(jax.random.fold_in(own, position), (shards_of,), jnp.float32, low / len(split), largest / len(split)))
        loudness = loudness * jnp.repeat(steps, dims[position] // shards_of).reshape([-1 if axis == position else 1 for axis in range(len(dims))])
    return loudness


def scatter_about(key, shape, spread, reach, split=(), kind=jnp.bfloat16):
    factor_of = level_of(key, shape, split, -0.22, 0.18) if split else 1.0
    array = jax.random.normal(key, shape, jnp.float32) * spread * factor_of
    return jnp.minimum(jnp.maximum(array, -reach), reach).astype(kind)


def setup_inputs(seed: int = 0, part: int = 0) -> dict:
    seeds = jax.random.split(jax.random.key(seed), 12)
    part_keys = jax.random.split(jax.random.fold_in(seeds[11], part), 12)
    return {
        "queries": draw_queries(jax.random.fold_in(jax.random.fold_in(seeds[11], part), 71), part),
        "keys": draw_keys(jax.random.fold_in(jax.random.fold_in(seeds[11], part), 71), part),
        "values": scatter_about(part_keys[2], (TOKENS, FEAT), 1.0, 6.0, ((0, 16),)),
        "q_gain": jnp.clip(jax.random.uniform(seeds[3], (FEAT,), jnp.float32, 1.2, 2.0), 1.2, 2.0),
        "k_gain": jnp.clip(jax.random.uniform(seeds[4], (FEAT,), jnp.float32, 1.2, 2.0), 1.2, 2.0),
        "prev_keys": draw_prev_keys(jax.random.fold_in(jax.random.fold_in(seeds[11], part), 71), part),
        "prev_values": scatter_about(part_keys[6], (TOKENS, FEAT), 1.0, 6.0, ((1, 4),)),
        "res_keys": scatter_about(part_keys[7], (SENT, BLK, FEAT), 0.5, 3.0, ((0, 4), (2, 4))),
        "res_values": scatter_about(part_keys[8], (SENT, BLK, FEAT), 0.5, 3.0, ((0, 4), (2, 4))),
        "block_ids": draw_block_ids(jax.random.fold_in(jax.random.fold_in(seeds[11], part), 71), part),
        "scale_exps": place_ends(jax.random.randint(part_keys[10], (SENT, HEADS), -2, 2), jax.random.fold_in(part_keys[10], 1), -2, 1).astype(jnp.int32),
    }


epsilon = 1e-06

def rms_scale(token_rows, gain_row):
    widened = token_rows.astype(jnp.float32)
    inverse = lax.rsqrt(lax.optimization_barrier(jnp.mean(widened * widened, axis=-1, keepdims=True)) + epsilon)
    return (widened * inverse * gain_row).astype(jnp.bfloat16)

def refresh_rows(stale_rows, residual, block_ids, exponents, sent_each):
    block_len = residual.shape[1]
    feature_count = stale_rows.shape[1]
    head_count = exponents.shape[1]
    blocks = stale_rows.reshape(stale_rows.shape[0] // block_len, block_len, feature_count)
    per_patch = blocks.shape[0] // (residual.shape[0] // sent_each)
    owner_patch = jnp.arange(residual.shape[0], dtype=jnp.int32) // sent_each
    where_to = (owner_patch * per_patch + block_ids).astype(jnp.int32)
    factor = jnp.repeat(jnp.exp2(exponents.astype(jnp.float32)), feature_count // head_count, axis=1)
    updated = blocks[where_to].astype(jnp.float32) + residual.astype(jnp.float32) * factor[:, None, :]
    return blocks.at[where_to].set(updated.astype(jnp.bfloat16)).reshape(stale_rows.shape)

def reference(queries, keys, values, q_gain, k_gain, prev_keys, prev_values, res_keys, res_values, block_ids, scale_exps):
    q_norm = rms_scale(queries, q_gain)
    k_norm = rms_scale(keys, k_gain)
    stale_keys = refresh_rows(prev_keys, res_keys, block_ids, scale_exps, SEND)
    stale_values = refresh_rows(prev_values, res_values, block_ids, scale_exps, SEND)
    root = jnp.zeros((), jnp.int32)

    def one_patch(patch_index):
        first_row = (patch_index * TOK_PATCH).astype(jnp.int32)
        own_keys = lax.dynamic_slice_in_dim(k_norm, first_row, TOK_PATCH, 0)
        own_values = lax.dynamic_slice_in_dim(values, first_row, TOK_PATCH, 0)
        key_set = lax.dynamic_update_slice(stale_keys, own_keys, (first_row, root))
        value_set = lax.dynamic_update_slice(stale_values, own_values, (first_row, root))
        query_rows = lax.dynamic_slice_in_dim(q_norm, first_row, TOK_PATCH, 0)
        query_heads = query_rows.astype(jnp.float32).reshape(TOK_PATCH, HEADS, HEAD_DIM)
        key_heads = key_set.astype(jnp.float32).reshape(TOKENS, HEADS, HEAD_DIM)
        value_heads = value_set.astype(jnp.float32).reshape(TOKENS, HEADS, HEAD_DIM)
        scores = jnp.einsum('qhd,khd->hqk', query_heads, key_heads) / math.sqrt(HEAD_DIM)
        peak = lax.optimization_barrier(jnp.max(scores, axis=-1, keepdims=True))
        powered = jnp.exp(scores - peak)
        denominator = lax.optimization_barrier(jnp.sum(powered, axis=-1))
        weights = lax.optimization_barrier(powered.astype(jnp.bfloat16)).astype(jnp.float32)
        summed = jnp.einsum('hqk,khd->qhd', weights, value_heads)
        result = summed / jnp.transpose(denominator)[:, :, None]
        return result.reshape(TOK_PATCH, HEADS * HEAD_DIM).astype(jnp.bfloat16)
    patch_count = TOKENS // TOK_PATCH
    outputs = lax.map(one_patch, jnp.arange(patch_count, dtype=jnp.int32))
    return outputs.reshape(TOKENS, HEADS * HEAD_DIM)
```

```python
import functools
import math

import jax
import jax.numpy as jnp
from jax import lax
from jax.experimental import pallas as pl
from jax.experimental.pallas import tpu as pltpu
from jax.sharding import PartitionSpec as P

epsilon = 1e-06
DIRECT_PATCHES = 8
VM = pl.BlockSpec(memory_space=pltpu.VMEM)
SM = pl.BlockSpec(memory_space=pltpu.SMEM)


def trade(array, axis, step, count):
    return lax.ppermute(array, axis, [(i, i ^ step) for i in range(count)])


def pack_kernel(sent, block_len, heads, size, tail, ids, exps, res_k, res_v, out):
    rows = sent * block_len
    for h in range(heads):
        for r in range(sent):
            power = (1 << (exps[r, h] + 16)).astype(jnp.float32) * (1.0 / 65536.0)
            lanes = pl.ds(h * size, size)
            k = res_k[r, :, lanes].astype(jnp.float32) * power
            v = res_v[r, :, lanes].astype(jnp.float32) * power
            out[pl.ds(h * 2 * rows + r * block_len, block_len), :] = k.astype(jnp.bfloat16)
            out[pl.ds((h * 2 + 1) * rows + r * block_len, block_len), :] = v.astype(jnp.bfloat16)
    lane = lax.broadcasted_iota(jnp.int32, (tail, size), 1) // block_len
    numbers = jnp.zeros((tail, size), jnp.float32)
    for r in range(sent):
        numbers = jnp.where(lane == r, ids[r].astype(jnp.float32), numbers)
    out[pl.ds(heads * 2 * rows, tail), :] = numbers.astype(jnp.bfloat16)


def norm_kernel(count, me, q_ref, k_ref, v_ref, qg_ref, kg_ref, *outs):
    rows, width = q_ref.shape[0], q_ref.shape[1] // count

    def inverse(ref):
        x = ref[...].astype(jnp.float32)
        return lax.rsqrt(jnp.mean(x * x, axis=-1, keepdims=True) + epsilon)

    q_inv, k_inv = inverse(q_ref), inverse(k_ref)
    for step in range(count):
        cols = pl.ds(pl.multiple_of((me[0] ^ step) * width, 128), width)
        q = q_ref[:, cols].astype(jnp.float32) * q_inv * qg_ref[:, cols]
        k = k_ref[:, cols].astype(jnp.float32) * k_inv * kg_ref[:, cols]
        outs[step][pl.ds(0, rows), :] = q.astype(jnp.bfloat16)
        outs[step][pl.ds(rows, rows), :] = k.astype(jnp.bfloat16)
        outs[step][pl.ds(2 * rows, rows), :] = v_ref[:, cols]


def attend_kernel(head_n, patch_n, direct, sent, block_len, size, me, *refs):
    parts = refs[:head_n]
    prev_k, prev_v = refs[head_n : head_n + 2]
    n_res = patch_n - 1 if direct else 1
    res = refs[head_n + 2 : head_n + 2 + n_res]
    outs = refs[head_n + 2 + n_res : head_n + 2 + n_res + head_n]
    q_all, k_all, v_all = refs[-3:]
    rows = parts[0].shape[0] // 3
    tok = rows * head_n
    width = parts[0].shape[1]
    heads = width // size
    fresh = sent * block_len

    for step in range(head_n):
        q_all[pl.ds(step * rows, rows), :] = parts[step][pl.ds(0, rows), :]
        k_all[pl.ds(step * rows, rows), :] = parts[step][pl.ds(rows, rows), :]
        v_all[pl.ds(step * rows, rows), :] = parts[step][pl.ds(2 * rows, rows), :]

    row = lax.broadcasted_iota(jnp.int32, (tok, fresh), 0)
    col = lax.broadcasted_iota(jnp.int32, (tok, fresh), 1)
    fits = row % block_len == col % block_len
    block = (row // block_len).astype(jnp.float32)

    def refresh(step, packed):
        owner = me[0] ^ step
        numbers = packed[pl.ds(heads * 2 * fresh, 16), :].astype(jnp.float32)[0:1, :fresh]
        chosen = jnp.logical_and(fits, block == numbers).astype(jnp.bfloat16)
        source = pl.ds(pl.multiple_of(owner * tok, 128), tok)
        target = pl.ds(pl.multiple_of(step * tok, 128), tok)
        for h in range(heads):
            lanes = pl.ds(h * size, size)
            for which, (old, new) in enumerate(((prev_k, k_all), (prev_v, v_all))):
                change = jnp.dot(
                    chosen,
                    packed[pl.ds((h * 2 + which) * fresh, fresh), :],
                    preferred_element_type=jnp.float32,
                )
                new[target, lanes] = (old[source, lanes].astype(jnp.float32) + change).astype(jnp.bfloat16)

    if direct:
        for step in range(1, patch_n):
            refresh(step, res[step - 1])
    else:

        @pl.loop(1, patch_n)
        def _(step):
            refresh(step, res[0].at[me[0] ^ step])

    for h in range(heads):
        lanes = pl.ds(h * size, size)
        scores = lax.dot_general(
            q_all[:, lanes], k_all[:, lanes], (((1,), (1,)), ((), ())), preferred_element_type=jnp.float32
        ) * (1.0 / math.sqrt(size))
        powered = jnp.exp(scores - jnp.max(scores, axis=-1, keepdims=True))
        total = jnp.sum(powered, axis=-1, keepdims=True)
        summed = jnp.dot(powered.astype(jnp.bfloat16), v_all[:, lanes], preferred_element_type=jnp.float32)
        result = (summed / total).astype(jnp.bfloat16)
        for step in range(head_n):
            outs[step][:, lanes] = result[step * rows : (step + 1) * rows]


def join_kernel(count, me, *refs):
    width = refs[0].shape[1]
    for step in range(count):
        cols = pl.ds(pl.multiple_of((me[0] ^ step) * width, 128), width)
        refs[count][:, cols] = refs[step][...]


def local(
    head_n,
    patch_n,
    queries,
    keys,
    values,
    q_gain,
    k_gain,
    prev_keys,
    prev_values,
    res_keys,
    res_values,
    block_ids,
    scale_exps,
):
    bf16 = jnp.bfloat16
    heads = scale_exps.shape[1]
    width = prev_keys.shape[1]
    size = width // heads
    sent, block_len = res_keys.shape[:2]
    rows = queries.shape[0]
    fresh = sent * block_len
    tail = 16
    my_head = lax.axis_index("head").reshape(1)
    my_patch = lax.axis_index("patch").reshape(1)
    direct = patch_n <= DIRECT_PATCHES

    packed = pl.pallas_call(
        functools.partial(pack_kernel, sent, block_len, heads, size, tail),
        out_shape=jax.ShapeDtypeStruct((heads * 2 * fresh + tail, size), bf16),
        in_specs=[SM, SM, VM, VM],
        out_specs=VM,
        name="pack",
    )(block_ids, scale_exps, res_keys, res_values)
    if direct:
        residuals = [trade(packed, "patch", step, patch_n) for step in range(1, patch_n)]
    else:
        residuals = [lax.all_gather(packed, "patch", axis=0)]

    parts = pl.pallas_call(
        functools.partial(norm_kernel, head_n),
        out_shape=[jax.ShapeDtypeStruct((3 * rows, width), bf16)] * head_n,
        in_specs=[SM] + [VM] * 5,
        out_specs=[VM] * head_n,
        name="norm",
    )(my_head, queries, keys, values, q_gain.reshape(1, -1), k_gain.reshape(1, -1))
    parts = [parts[0]] + [trade(parts[step], "head", step, head_n) for step in range(1, head_n)]

    tok = rows * head_n
    total = tok * patch_n
    outs = pl.pallas_call(
        functools.partial(attend_kernel, head_n, patch_n, direct, sent, block_len, size),
        out_shape=[jax.ShapeDtypeStruct((rows, width), bf16)] * head_n,
        in_specs=[SM] + [VM] * (head_n + 2 + len(residuals)),
        out_specs=[VM] * head_n,
        scratch_shapes=[
            pltpu.VMEM((tok, width), bf16),
            pltpu.VMEM((total, width), bf16),
            pltpu.VMEM((total, width), bf16),
        ],
        compiler_params=pltpu.CompilerParams(vmem_limit_bytes=(16 if direct else 48) * 2**20),
        name="attend",
    )(my_patch, *parts, prev_keys, prev_values, *residuals)
    outs = [outs[0]] + [trade(outs[step], "head", step, head_n) for step in range(1, head_n)]
    return pl.pallas_call(
        functools.partial(join_kernel, head_n),
        out_shape=jax.ShapeDtypeStruct((rows, width * head_n), bf16),
        in_specs=[SM] + [VM] * head_n,
        out_specs=VM,
        name="join",
    )(my_head, *outs)


def solution(mesh):
    in_specs = (
        P(("groups", "patch", "head"), None),
        P(("groups", "patch", "head"), None),
        P(("groups", "patch", "head"), None),
        P(),
        P(),
        P("groups", "head"),
        P("groups", "head"),
        P(("groups", "patch"), None, "head"),
        P(("groups", "patch"), None, "head"),
        P(("groups", "patch")),
        P(("groups", "patch"), "head"),
    )
    out_specs = P(("groups", "patch", "head"), None)
    body = functools.partial(local, mesh.shape["head"], mesh.shape["patch"])
    return jax.shard_map(body, mesh=mesh, in_specs=in_specs, out_specs=out_specs, check_vma=False)
```

```python
import functools
import math

import jax
import jax.numpy as jnp
from jax import lax
from jax.experimental import pallas as pl
from jax.experimental.pallas import tpu as pltpu
from jax.sharding import PartitionSpec as P

epsilon = 1e-06
VM = pl.BlockSpec(memory_space=pltpu.VMEM)
SM = pl.BlockSpec(memory_space=pltpu.SMEM)


def trade(array, axis, step, count):
    return lax.ppermute(array, axis, [(i, i ^ step) for i in range(count)])


def pack(sent, block_len, heads, size, tail, ids, exps, res_k, res_v, out):
    rows = sent * block_len
    for h in range(heads):
        for r in range(sent):
            power = (1 << (exps[r, h] + 16)).astype(jnp.float32) * (1.0 / 65536.0)
            lanes = pl.ds(h * size, size)
            k = res_k[r, :, lanes].astype(jnp.float32) * power
            v = res_v[r, :, lanes].astype(jnp.float32) * power
            out[pl.ds(h * 2 * rows + r * block_len, block_len), :] = k.astype(jnp.bfloat16)
            out[pl.ds((h * 2 + 1) * rows + r * block_len, block_len), :] = v.astype(jnp.bfloat16)
    lane = lax.broadcasted_iota(jnp.int32, (tail, size), 1) // block_len
    numbers = jnp.zeros((tail, size), jnp.float32)
    for r in range(sent):
        numbers = jnp.where(lane == r, ids[r].astype(jnp.float32), numbers)
    out[pl.ds(heads * 2 * rows, tail), :] = numbers.astype(jnp.bfloat16)


def prepare_kernel(count, sent, block_len, heads, size, tail, n_in, me, *refs):
    inputs, out, outs = refs[:n_in], refs[n_in], refs[n_in + 1 : n_in + 1 + count]
    held, sems = refs[n_in + 1 + count : -1], refs[-1]
    copies = [pltpu.make_async_copy(a, b, sems.at[i]) for i, (a, b) in enumerate(zip(inputs, held, strict=True))]
    for copy in copies:
        copy.start()
    ids, exps, res_k, res_v, q_ref, qg_ref, k_ref, kg_ref, v_ref = held
    for copy in copies[:4]:
        copy.wait()
    pack(sent, block_len, heads, size, tail, ids, exps, res_k, res_v, out)
    rows, width = q_ref.shape[0], q_ref.shape[1] // count
    columns = [pl.ds(pl.multiple_of((me[0] ^ step) * width, 128), width) for step in range(count)]
    for at, (ref, gain) in enumerate(((q_ref, qg_ref), (k_ref, kg_ref))):
        copies[4 + 2 * at].wait()
        copies[5 + 2 * at].wait()
        x = ref[...].astype(jnp.float32)
        inverse = lax.rsqrt(jnp.mean(x * x, axis=-1, keepdims=True) + epsilon)
        for step, cols in enumerate(columns):
            normal = ref[:, cols].astype(jnp.float32) * inverse * gain[cols]
            outs[step][pl.ds(at * rows, rows), :] = normal.astype(jnp.bfloat16)
    copies[8].wait()
    for step, cols in enumerate(columns):
        outs[step][pl.ds(2 * rows, rows), :] = v_ref[:, cols]


def stage_kernel(k_ref, v_ref, k_out, v_out, sems):
    copies = [pltpu.make_async_copy(k_ref, k_out, sems.at[0]), pltpu.make_async_copy(v_ref, v_out, sems.at[1])]
    for copy in copies:
        copy.start()
    for copy in copies:
        copy.wait()


def attend_kernel(head_n, patch_n, direct, sent, block_len, size, me, *refs):
    parts = refs[:head_n]
    prev_k, prev_v = refs[head_n : head_n + 2]
    n_res = patch_n - 1 if direct else 1
    res = refs[head_n + 2 : head_n + 2 + n_res]
    outs = refs[head_n + 2 + n_res : head_n + 2 + n_res + head_n]
    q_all, k_all, v_all = refs[-3:]
    rows = parts[0].shape[0] // 3
    tok = rows * head_n
    width = parts[0].shape[1]
    heads = width // size
    fresh = sent * block_len

    for step in range(head_n):
        q_all[pl.ds(step * rows, rows), :] = parts[step][pl.ds(0, rows), :]
        k_all[pl.ds(step * rows, rows), :] = parts[step][pl.ds(rows, rows), :]
        v_all[pl.ds(step * rows, rows), :] = parts[step][pl.ds(2 * rows, rows), :]

    row = lax.broadcasted_iota(jnp.int32, (tok, fresh), 0)
    col = lax.broadcasted_iota(jnp.int32, (tok, fresh), 1)
    fits = row % block_len == col % block_len
    block = (row // block_len).astype(jnp.float32)

    def refresh(step, packed):
        owner = me[0] ^ step
        numbers = packed[pl.ds(heads * 2 * fresh, 16), :].astype(jnp.float32)[0:1, :fresh]
        chosen = jnp.logical_and(fits, block == numbers).astype(jnp.bfloat16)
        source = pl.ds(pl.multiple_of(owner * tok, 128), tok)
        target = pl.ds(pl.multiple_of(step * tok, 128), tok)
        for h in range(heads):
            lanes = pl.ds(h * size, size)
            for which, (old, new) in enumerate(((prev_k, k_all), (prev_v, v_all))):
                change = jnp.dot(
                    chosen,
                    packed[pl.ds((h * 2 + which) * fresh, fresh), :],
                    preferred_element_type=jnp.float32,
                )
                new[target, lanes] = (old[source, lanes].astype(jnp.float32) + change).astype(jnp.bfloat16)

    if direct:
        for step in range(1, patch_n):
            refresh(step, res[step - 1])
    else:

        @pl.loop(1, patch_n)
        def _(step):
            refresh(step, res[0].at[me[0] ^ step])

    for h in range(heads):
        lanes = pl.ds(h * size, size)
        scores = lax.dot_general(
            q_all[:, lanes], k_all[:, lanes], (((1,), (1,)), ((), ())), preferred_element_type=jnp.float32
        ) * (1.0 / math.sqrt(size))
        powered = jnp.exp(scores - jnp.max(scores, axis=-1, keepdims=True))
        total = jnp.sum(powered, axis=-1, keepdims=True)
        summed = jnp.dot(powered.astype(jnp.bfloat16), v_all[:, lanes], preferred_element_type=jnp.float32)
        result = (summed / total).astype(jnp.bfloat16)
        for step in range(head_n):
            outs[step][:, lanes] = result[step * rows : (step + 1) * rows]


def join_kernel(count, me, *refs):
    width = refs[0].shape[1]
    for step in range(count):
        cols = pl.ds(pl.multiple_of((me[0] ^ step) * width, 128), width)
        refs[count][:, cols] = refs[step][...]


def local(
    head_n,
    patch_n,
    queries,
    keys,
    values,
    q_gain,
    k_gain,
    prev_keys,
    prev_values,
    res_keys,
    res_values,
    block_ids,
    scale_exps,
):
    bf16 = jnp.bfloat16
    heads = scale_exps.shape[1]
    width = prev_keys.shape[1]
    size = width // heads
    sent, block_len = res_keys.shape[:2]
    rows = queries.shape[0]
    fresh = sent * block_len
    tail = 16
    my_head = lax.axis_index("head").reshape(1)
    my_patch = lax.axis_index("patch").reshape(1)
    direct = patch_n == 4

    small = pltpu.CompilerParams(vmem_limit_bytes=8 * 2**20)
    hbm = pl.BlockSpec(memory_space=pltpu.HBM)
    in_hbm = functools.partial(pltpu.with_memory_space_constraint, memory_space=pltpu.HBM)
    inputs = (block_ids, scale_exps, res_keys, res_values, queries, q_gain, keys, k_gain, values)
    packed, *parts = pl.pallas_call(
        functools.partial(prepare_kernel, head_n, sent, block_len, heads, size, tail, len(inputs)),
        out_shape=[jax.ShapeDtypeStruct((heads * 2 * fresh + tail, size), bf16)]
        + [jax.ShapeDtypeStruct((3 * rows, width), bf16)] * head_n,
        in_specs=[SM] + [hbm] * len(inputs),
        out_specs=[VM] * (head_n + 1),
        scratch_shapes=[pltpu.SMEM(x.shape, x.dtype) for x in inputs[:2]]
        + [pltpu.VMEM(x.shape, x.dtype) for x in inputs[2:]]
        + [pltpu.SemaphoreType.DMA((len(inputs),))],
        compiler_params=small,
        name="prepare",
    )(my_head, *[in_hbm(x) for x in inputs])
    prev_keys, prev_values = pl.pallas_call(
        stage_kernel,
        out_shape=[jax.ShapeDtypeStruct(prev_keys.shape, bf16)] * 2,
        in_specs=[hbm] * 2,
        out_specs=[VM] * 2,
        scratch_shapes=[pltpu.SemaphoreType.DMA((2,))],
        compiler_params=pltpu.CompilerParams(vmem_limit_bytes=(8 if patch_n == 4 else 16) * 2**20),
        cost_estimate=pl.CostEstimate(flops=0, bytes_accessed=4 * prev_keys.size, transcendentals=0),
        name="stage",
    )(in_hbm(prev_keys), in_hbm(prev_values))
    if patch_n == 4:
        far = trade(packed, "patch", 2, patch_n)
        parts = [parts[0]] + [trade(parts[step], "head", step, head_n) for step in range(1, head_n)]
        near = trade(packed, "patch", 1, patch_n)
        residuals = [near, far, trade(far, "patch", 1, patch_n)]
    else:
        parts = [parts[0]] + [trade(parts[step], "head", step, head_n) for step in range(1, head_n)]
        residuals = [lax.all_gather(packed, "patch", axis=0)]

    tok = rows * head_n
    total = tok * patch_n
    outs = pl.pallas_call(
        functools.partial(attend_kernel, head_n, patch_n, direct, sent, block_len, size),
        out_shape=[jax.ShapeDtypeStruct((rows, width), bf16)] * head_n,
        in_specs=[SM] + [VM] * (head_n + 2 + len(residuals)),
        out_specs=[VM] * head_n,
        scratch_shapes=[
            pltpu.VMEM((tok, width), bf16),
            pltpu.VMEM((total, width), bf16),
            pltpu.VMEM((total, width), bf16),
        ],
        compiler_params=pltpu.CompilerParams(vmem_limit_bytes=(8 if direct else 48) * 2**20),
        name="attend",
    )(my_patch, *parts, prev_keys, prev_values, *residuals)
    outs = [outs[0]] + [trade(outs[step], "head", step, head_n) for step in range(1, head_n)]
    return pl.pallas_call(
        functools.partial(join_kernel, head_n),
        out_shape=jax.ShapeDtypeStruct((rows, width * head_n), bf16),
        in_specs=[SM] + [VM] * head_n,
        out_specs=VM,
        compiler_params=small,
        name="join",
    )(my_head, *outs)


def solution(mesh):
    in_specs = (
        P(("groups", "patch", "head"), None),
        P(("groups", "patch", "head"), None),
        P(("groups", "patch", "head"), None),
        P(),
        P(),
        P("groups", "head"),
        P("groups", "head"),
        P(("groups", "patch"), None, "head"),
        P(("groups", "patch"), None, "head"),
        P(("groups", "patch")),
        P(("groups", "patch"), "head"),
    )
    out_specs = P(("groups", "patch", "head"), None)
    body = functools.partial(local, mesh.shape["head"], mesh.shape["patch"])
    return jax.shard_map(body, mesh=mesh, in_specs=in_specs, out_specs=out_specs, check_vma=False)
```

```python
import functools
import math

import jax
import jax.numpy as jnp
from jax import lax
from jax.experimental import pallas as pl
from jax.experimental.pallas import tpu as pltpu
from jax.sharding import PartitionSpec as P

epsilon = 1e-06
tail = 16
VM = pl.BlockSpec(memory_space=pltpu.VMEM)
SM = pl.BlockSpec(memory_space=pltpu.SMEM)
HB = pl.BlockSpec(memory_space=pltpu.HBM)
in_hbm = functools.partial(pltpu.with_memory_space_constraint, memory_space=pltpu.HBM)


def trade(array, axis, step, count):
    return lax.ppermute(array, axis, [(i, i ^ step) for i in range(count)])


def order_of(count):
    return [*range(2, count), *range(min(2, count))]


def in_turn(refs):
    turned = dict(zip(order_of(len(refs)), refs, strict=True))
    return [turned[step] for step in range(len(refs))]


def start_all(pairs, sems):
    copies = [pltpu.make_async_copy(a, b, sems.at[i]) for i, (a, b) in enumerate(pairs)]
    for copy in copies:
        copy.start()
    return copies


def prepare_kernel(count, n_in, me, *refs):
    inputs, both, outs = refs[:n_in], refs[n_in], refs[n_in + 1 : n_in + 1 + count]
    held, sems = refs[n_in + 1 + count : -1], refs[-1]
    copies = start_all(zip(inputs, held, strict=True), sems)
    ids, exps, res_k, res_v, q_ref, qg_ref, k_ref, kg_ref, v_ref = held

    sent, block_len = res_k.shape[:2]
    heads = exps.shape[1]
    size = res_k.shape[2] // heads
    after = heads * sent * block_len + tail
    for copy in copies[:4]:
        copy.wait()
    for h in range(heads):
        for r in range(sent):
            power = (1 << (exps[r, h] + 16)).astype(jnp.float32) * (1.0 / 65536.0)
            lanes = pl.ds(h * size, size)
            at = (h * sent + r) * block_len
            k = (res_k[r, :, lanes].astype(jnp.float32) * power).astype(jnp.bfloat16)
            v = (res_v[r, :, lanes].astype(jnp.float32) * power).astype(jnp.bfloat16)
            both[pl.ds(at, block_len), :] = k
            both[pl.ds(after + at, block_len), :] = v
    lane = lax.broadcasted_iota(jnp.int32, (tail, size), 1) // block_len
    numbers = jnp.zeros((tail, size), jnp.float32)
    for r in range(sent):
        numbers = jnp.where(lane == r, ids[r].astype(jnp.float32), numbers)
    both[pl.ds(after - tail, tail), :] = numbers.astype(jnp.bfloat16)

    rows, width = q_ref.shape[0], q_ref.shape[1] // count
    columns = [pl.ds(pl.multiple_of((me[0] ^ step) * width, 128), width) for step in range(count)]
    for at, (ref, gain) in enumerate(((q_ref, qg_ref), (k_ref, kg_ref))):
        copies[4 + 2 * at].wait()
        copies[5 + 2 * at].wait()
        x = ref[...].astype(jnp.float32)
        inverse = lax.rsqrt(jnp.mean(x * x, axis=-1, keepdims=True) + epsilon)
        for step, cols in enumerate(columns):
            normal = ref[:, cols].astype(jnp.float32) * inverse * gain[cols]
            outs[step][pl.ds(at * rows, rows), :] = normal.astype(jnp.bfloat16)
    copies[8].wait()
    for step, cols in enumerate(columns):
        outs[step][pl.ds(2 * rows, rows), :] = v_ref[:, cols]


def chooser(tok, fresh, block_len, packed_k, rows_k):
    row = lax.broadcasted_iota(jnp.int32, (tok, fresh), 0)
    col = lax.broadcasted_iota(jnp.int32, (tok, fresh), 1)
    numbers = packed_k[pl.ds(rows_k, tail), :].astype(jnp.float32)[0:1, :fresh]
    return jnp.logical_and(
        row % block_len == col % block_len, (row // block_len).astype(jnp.float32) == numbers
    ).astype(jnp.bfloat16)


def refresh(chosen, old, source, new, target, residual, first):
    fresh = chosen.shape[1]
    size = residual.shape[1]
    for h in range(new.shape[1] // size):
        lanes = pl.ds(h * size, size)
        change = jnp.dot(
            chosen, residual[pl.ds(first + h * fresh, fresh), :], preferred_element_type=jnp.float32
        )
        new[target, lanes] = (old[source, lanes].astype(jnp.float32) + change).astype(jnp.bfloat16)


def stage_kernel(steps, early, tok, fresh, block_len, n_res, me, k_ref, v_ref, *refs):
    res, (k_out, v_out, sems) = refs[:n_res], refs[n_res:]
    pairs = []
    for place, step in enumerate(steps):
        source = pl.ds(pl.multiple_of((me[0] ^ step) * tok, 128), tok)
        target = pl.ds(place * tok, tok)
        pairs += [(k_ref.at[source], k_out.at[target]), (v_ref.at[source], v_out.at[target])]
    copies = start_all(pairs, sems)
    rows_k = k_out.shape[1] // res[0].shape[-1] * fresh

    def one(place, packed):
        rows = place * tok
        rows = pl.ds(rows if isinstance(place, int) else pl.multiple_of(rows, 128), tok)
        chosen = chooser(tok, fresh, block_len, packed, rows_k)
        refresh(chosen, k_out, rows, k_out, rows, packed, 0)
        refresh(chosen, v_out, rows, v_out, rows, packed, rows_k + tail)

    for copy in copies:
        copy.wait()
    if early:
        for place in range(early):
            one(place, res[place])
    else:

        @pl.loop(1, len(steps) + 1)
        def _(step):
            one(step - 1, res[0].at[me[0] ^ step])


def scored(q, keys):
    return lax.dot_general(
        q, keys, (((1,), (1,)), ((), ())), preferred_element_type=jnp.float32
    ) * (math.log2(math.e) / math.sqrt(q.shape[1]))


def score_kernel(count, n_now, ahead, block_len, fresh, size, *refs):
    (k_st, v_st), now, parts = refs[:2], refs[2 : 2 + n_now], in_turn(refs[2 + n_now : 2 + n_now + count])
    q_all, v_own, scores, k_own = refs[2 + n_now + count :]
    rows = parts[0].shape[0] // 3
    tok = rows * count
    heads = parts[0].shape[1] // size
    for place, packed in enumerate(now):
        chosen = chooser(tok, fresh, block_len, packed, heads * fresh)
        source, target = pl.ds(ahead + place * tok, tok), pl.ds((1 + place) * tok, tok)
        refresh(chosen, k_st, source, k_own, target, packed, 0)
        refresh(chosen, v_st, source, v_own, target, packed, heads * fresh + tail)
    for step in range(count):
        q_all[pl.ds(step * rows, rows), :] = parts[step][pl.ds(0, rows), :]
        k_own[pl.ds(step * rows, rows), :] = parts[step][pl.ds(rows, rows), :]
        v_own[pl.ds(step * rows, rows), :] = parts[step][pl.ds(2 * rows, rows), :]
    for h in range(heads):
        lanes = pl.ds(h * size, size)
        scores[h, :, pl.ds(0, ahead)] = scored(q_all[:, lanes], k_st[pl.ds(0, ahead), lanes])
        scores[h, :, pl.ds(ahead, k_own.shape[0])] = scored(q_all[:, lanes], k_own[:, lanes])


def finish_kernel(count, n_late, ahead, block_len, fresh, size, *refs):
    (k_st, v_st, q_all, v_own, scores), late = refs[:5], refs[5 : 5 + n_late]
    outs, (k_new, v_new) = refs[5 + n_late : -2], refs[-2:]
    tok = q_all.shape[0]
    rows = tok // count
    heads = q_all.shape[1] // size
    for packed in late:
        chosen = chooser(tok, fresh, block_len, packed, heads * fresh)
        source, target = pl.ds(k_st.shape[0] - tok, tok), pl.ds(0, tok)
        refresh(chosen, k_st, source, k_new, target, packed, 0)
        refresh(chosen, v_st, source, v_new, target, packed, heads * fresh + tail)
    columns = [pl.ds(h * size, size) for h in range(heads)]
    together = heads if late else 1
    for first in range(0, heads, together):
        group = range(first, first + together)
        cut = {h: [scores[h, :, pl.ds(0, ahead)], scores[h, :, pl.ds(ahead, v_own.shape[0])]] for h in group}
        held = {h: [v_st[pl.ds(0, ahead), columns[h]], v_own[:, columns[h]]] for h in group}
        if late:
            for h in group:
                cut[h].append(scored(q_all[:, columns[h]], k_new[:, columns[h]]))
                held[h].append(v_new[:, columns[h]])
        peaks = {h: row_fold(jnp.maximum, jnp.max, cut[h]) for h in group}
        powered, summed = {}, {}
        for h in group:
            powered[h] = [jnp.exp2(part - peaks[h]) for part in cut[h]]
            summed[h] = jnp.dot(
                jnp.concatenate([part.astype(jnp.bfloat16) for part in powered[h]], axis=1),
                jnp.concatenate(held[h], axis=0),
                preferred_element_type=jnp.float32,
            )
        totals = {h: row_fold(jnp.add, jnp.sum, powered[h]) for h in group}
        for h in group:
            result = (summed[h] / totals[h]).astype(jnp.bfloat16)
            for step in range(count):
                outs[step][:, columns[h]] = result[step * rows : (step + 1) * rows]


def row_fold(both, along, parts):
    blocks = [part[:, at : at + 128] for part in parts for at in range(0, part.shape[1], 128)]
    return along(functools.reduce(both, blocks), axis=-1, keepdims=True)


def join_kernel(count, me, *refs):
    parts, out = in_turn(refs[:count]), refs[count]
    width = parts[0].shape[1]
    for step in range(count):
        out[:, pl.ds(pl.multiple_of((me[0] ^ step) * width, 128), width)] = parts[step][...]


def local(
    head_n,
    patch_n,
    queries,
    keys,
    values,
    q_gain,
    k_gain,
    prev_keys,
    prev_values,
    res_keys,
    res_values,
    block_ids,
    scale_exps,
):
    bf16 = jnp.bfloat16
    heads = scale_exps.shape[1]
    width = prev_keys.shape[1]
    size = width // heads
    sent, block_len = res_keys.shape[:2]
    rows = queries.shape[0]
    tok = rows * head_n
    fresh = sent * block_len
    my_head = lax.axis_index("head").reshape(1)
    my_patch = lax.axis_index("patch").reshape(1)
    four = patch_n == 4
    grant = pltpu.CompilerParams(vmem_limit_bytes=8 * 2**20)
    larger = grant if four else pltpu.CompilerParams(vmem_limit_bytes=24 * 2**20)

    def shape(*dims):
        return jax.ShapeDtypeStruct(dims, bf16)

    inputs = (block_ids, scale_exps, res_keys, res_values, queries, q_gain, keys, k_gain, values)
    both, *parts = pl.pallas_call(
        functools.partial(prepare_kernel, head_n, len(inputs)),
        out_shape=[shape(2 * heads * fresh + tail, size)] + [shape(3 * rows, width)] * head_n,
        in_specs=[SM] + [HB] * len(inputs),
        out_specs=[VM] * (head_n + 1),
        scratch_shapes=[pltpu.SMEM(x.shape, x.dtype) for x in inputs[:2]]
        + [pltpu.VMEM(x.shape, x.dtype) for x in inputs[2:]]
        + [pltpu.SemaphoreType.DMA((len(inputs),))],
        compiler_params=grant,
        name="prepare",
    )(my_head, *[in_hbm(x) for x in inputs])

    if four:
        near = trade(both, "patch", 1, patch_n)
        far = trade(both, "patch", 2, patch_n)
        residuals = [far]
        steps, late = [2, 1, 3], [near]
    else:
        residuals = [lax.all_gather(both, "patch", axis=0)]
        steps, late = range(1, patch_n), []
    order = order_of(head_n)
    parts = [trade(parts[step], "head", step, head_n) if step else parts[0] for step in range(head_n)]
    now = late
    late = [trade(far, "patch", 1, patch_n)] if four else []

    others = (patch_n - 1) * tok
    stale_k, stale_v = pl.pallas_call(
        functools.partial(stage_kernel, steps, 1 if four else 0, tok, fresh, block_len, len(residuals)),
        out_shape=[shape(others, width)] * 2,
        in_specs=[SM] + [HB] * 2 + [VM] * len(residuals),
        out_specs=[VM] * 2,
        scratch_shapes=[pltpu.SemaphoreType.DMA((2 * (patch_n - 1),))],
        compiler_params=larger,
        name="stage",
    )(my_patch, in_hbm(prev_keys), in_hbm(prev_values), *residuals)

    ahead = others - (len(now) + len(late)) * tok
    own = (1 + len(now)) * tok
    kept = jax.ShapeDtypeStruct((heads, tok, ahead + own), jnp.float32)
    q_all, v_own, scores = pl.pallas_call(
        functools.partial(score_kernel, head_n, len(now), ahead, block_len, fresh, size),
        out_shape=[shape(tok, width), shape(own, width), kept],
        in_specs=[VM] * (head_n + 2 + len(now)),
        out_specs=[VM] * 3,
        scratch_shapes=[pltpu.VMEM((own, width), bf16)],
        compiler_params=larger,
        name="score",
    )(stale_k, stale_v, *now, *[parts[step] for step in order])
    outs = pl.pallas_call(
        functools.partial(finish_kernel, head_n, len(late), ahead, block_len, fresh, size),
        out_shape=[shape(rows, width)] * head_n,
        in_specs=[VM] * (5 + len(late)),
        out_specs=[VM] * head_n,
        scratch_shapes=[pltpu.VMEM((tok, width), bf16)] * 2,
        compiler_params=larger,
        name="finish",
    )(stale_k, stale_v, q_all, v_own, scores, *late)
    outs = [trade(outs[step], "head", step, head_n) if step else outs[0] for step in range(head_n)]
    return pl.pallas_call(
        functools.partial(join_kernel, head_n),
        out_shape=shape(rows, width * head_n),
        in_specs=[SM] + [VM] * head_n,
        out_specs=VM,
        compiler_params=grant,
        name="join",
    )(my_head, *[outs[step] for step in order])


def solution(mesh):
    in_specs = (
        P(("groups", "patch", "head"), None),
        P(("groups", "patch", "head"), None),
        P(("groups", "patch", "head"), None),
        P(),
        P(),
        P("groups", "head"),
        P("groups", "head"),
        P(("groups", "patch"), None, "head"),
        P(("groups", "patch"), None, "head"),
        P(("groups", "patch")),
        P(("groups", "patch"), "head"),
    )
    out_specs = P(("groups", "patch", "head"), None)
    body = functools.partial(local, mesh.shape["head"], mesh.shape["patch"])
    return jax.shard_map(body, mesh=mesh, in_specs=in_specs, out_specs=out_specs, check_vma=False)
```

```python
import functools
import math

import jax
import jax.numpy as jnp
from jax import lax
from jax.experimental import pallas as pl
from jax.experimental.pallas import tpu as pltpu
from jax.sharding import PartitionSpec as P

epsilon = 1e-06
tail = 16
VM = pl.BlockSpec(memory_space=pltpu.VMEM)
SM = pl.BlockSpec(memory_space=pltpu.SMEM)
HB = pl.BlockSpec(memory_space=pltpu.HBM)
in_hbm = functools.partial(pltpu.with_memory_space_constraint, memory_space=pltpu.HBM)


def trade(array, axis, step, count):
    return lax.ppermute(array, axis, [(i, i ^ step) for i in range(count)])


def tokens_in(count):
    return [*range(2, count), *range(min(2, count))]


def tokens_out(count):
    return list(reversed(range(count)))


def in_turn(refs, order):
    turned = dict(zip(order(len(refs)), refs, strict=True))
    return [turned[step] for step in range(len(refs))]


def start_all(pairs, sems):
    copies = [pltpu.make_async_copy(a, b, sems.at[i]) for i, (a, b) in enumerate(pairs)]
    for copy in copies:
        copy.start()
    return copies


def prepare_kernel(count, n_in, me, *refs):
    inputs, both, outs = refs[:n_in], refs[n_in], refs[n_in + 1 : n_in + 1 + count]
    held, sems = refs[n_in + 1 + count : -1], refs[-1]
    copies = start_all(zip(inputs, held, strict=True), sems)
    ids, exps, res_k, res_v, q_ref, qg_ref, k_ref, kg_ref, v_ref = held

    sent, block_len = res_k.shape[:2]
    heads = exps.shape[1]
    size = res_k.shape[2] // heads
    after = heads * sent * block_len + tail
    for copy in copies[:4]:
        copy.wait()
    for h in range(heads):
        for r in range(sent):
            power = (1 << (exps[r, h] + 16)).astype(jnp.float32) * (1.0 / 65536.0)
            lanes = pl.ds(h * size, size)
            at = (h * sent + r) * block_len
            k = (res_k[r, :, lanes].astype(jnp.float32) * power).astype(jnp.bfloat16)
            v = (res_v[r, :, lanes].astype(jnp.float32) * power).astype(jnp.bfloat16)
            both[pl.ds(at, block_len), :] = k
            both[pl.ds(after + at, block_len), :] = v
    lane = lax.broadcasted_iota(jnp.int32, (tail, size), 1) // block_len
    numbers = jnp.zeros((tail, size), jnp.float32)
    for r in range(sent):
        numbers = jnp.where(lane == r, ids[r].astype(jnp.float32), numbers)
    both[pl.ds(after - tail, tail), :] = numbers.astype(jnp.bfloat16)

    rows, width = q_ref.shape[0], q_ref.shape[1] // count
    columns = [pl.ds(pl.multiple_of((me[0] ^ step) * width, 128), width) for step in range(count)]
    for at, (ref, gain) in enumerate(((q_ref, qg_ref), (k_ref, kg_ref))):
        copies[4 + 2 * at].wait()
        copies[5 + 2 * at].wait()
        x = ref[...].astype(jnp.float32)
        inverse = lax.rsqrt(jnp.mean(x * x, axis=-1, keepdims=True) + epsilon)
        for step, cols in enumerate(columns):
            normal = ref[:, cols].astype(jnp.float32) * inverse * gain[cols]
            outs[step][pl.ds(at * rows, rows), :] = normal.astype(jnp.bfloat16)
    copies[8].wait()
    for step, cols in enumerate(columns):
        outs[step][pl.ds(2 * rows, rows), :] = v_ref[:, cols]


def chooser(tok, fresh, block_len, packed_k, rows_k):
    row = lax.broadcasted_iota(jnp.int32, (tok, fresh), 0)
    col = lax.broadcasted_iota(jnp.int32, (tok, fresh), 1)
    numbers = packed_k[pl.ds(rows_k, tail), :].astype(jnp.float32)[0:1, :fresh]
    return jnp.logical_and(
        row % block_len == col % block_len, (row // block_len).astype(jnp.float32) == numbers
    ).astype(jnp.bfloat16)


def refresh(chosen, old, source, new, target, residual, first):
    fresh = chosen.shape[1]
    size = residual.shape[1]
    for h in range(new.shape[1] // size):
        lanes = pl.ds(h * size, size)
        change = jnp.dot(
            chosen, residual[pl.ds(first + h * fresh, fresh), :], preferred_element_type=jnp.float32
        )
        new[target, lanes] = (old[source, lanes].astype(jnp.float32) + change).astype(jnp.bfloat16)


def stage_kernel(steps, early, tok, fresh, block_len, n_res, me, k_ref, v_ref, *refs):
    res, (k_out, v_out, sems) = refs[:n_res], refs[n_res:]
    pairs = []
    for place, step in enumerate(steps):
        source = pl.ds(pl.multiple_of((me[0] ^ step) * tok, 128), tok)
        target = pl.ds(place * tok, tok)
        pairs += [(k_ref.at[source], k_out.at[target]), (v_ref.at[source], v_out.at[target])]
    copies = start_all(pairs, sems)
    rows_k = k_out.shape[1] // res[0].shape[-1] * fresh

    def one(place, packed):
        rows = place * tok
        rows = pl.ds(rows if isinstance(place, int) else pl.multiple_of(rows, 128), tok)
        chosen = chooser(tok, fresh, block_len, packed, rows_k)
        refresh(chosen, k_out, rows, k_out, rows, packed, 0)
        refresh(chosen, v_out, rows, v_out, rows, packed, rows_k + tail)

    for copy in copies:
        copy.wait()
    if early:
        for place in range(early):
            one(place, res[place])
    else:

        @pl.loop(1, len(steps) + 1)
        def _(step):
            one(step - 1, res[0].at[me[0] ^ step])


def scored(q, keys):
    return lax.dot_general(
        q, keys, (((1,), (1,)), ((), ())), preferred_element_type=jnp.float32
    ) * (math.log2(math.e) / math.sqrt(q.shape[1]))


def score_kernel(count, n_now, ahead, block_len, fresh, size, *refs):
    (k_st, v_st), now, parts = refs[:2], refs[2 : 2 + n_now], in_turn(refs[2 + n_now : 2 + n_now + count], tokens_in)
    q_all, v_own, scores, k_own = refs[2 + n_now + count :]
    rows = parts[0].shape[0] // 3
    tok = rows * count
    heads = parts[0].shape[1] // size
    for place, packed in enumerate(now):
        chosen = chooser(tok, fresh, block_len, packed, heads * fresh)
        source, target = pl.ds(ahead + place * tok, tok), pl.ds((1 + place) * tok, tok)
        refresh(chosen, k_st, source, k_own, target, packed, 0)
        refresh(chosen, v_st, source, v_own, target, packed, heads * fresh + tail)
    for step in range(count):
        q_all[pl.ds(step * rows, rows), :] = parts[step][pl.ds(0, rows), :]
        k_own[pl.ds(step * rows, rows), :] = parts[step][pl.ds(rows, rows), :]
        v_own[pl.ds(step * rows, rows), :] = parts[step][pl.ds(2 * rows, rows), :]
    for h in range(heads):
        lanes = pl.ds(h * size, size)
        scores[h, :, pl.ds(0, ahead)] = scored(q_all[:, lanes], k_st[pl.ds(0, ahead), lanes])
        scores[h, :, pl.ds(ahead, k_own.shape[0])] = scored(q_all[:, lanes], k_own[:, lanes])


def finish_kernel(count, n_late, ahead, block_len, fresh, size, *refs):
    (k_st, v_st, q_all, v_own, scores), late = refs[:5], refs[5 : 5 + n_late]
    outs, (k_new, v_new) = refs[5 + n_late : -2], refs[-2:]
    tok = q_all.shape[0]
    rows = tok // count
    heads = q_all.shape[1] // size
    for packed in late:
        chosen = chooser(tok, fresh, block_len, packed, heads * fresh)
        source, target = pl.ds(k_st.shape[0] - tok, tok), pl.ds(0, tok)
        refresh(chosen, k_st, source, k_new, target, packed, 0)
        refresh(chosen, v_st, source, v_new, target, packed, heads * fresh + tail)
    columns = [pl.ds(h * size, size) for h in range(heads)]
    together = heads if late else 1
    for first in range(0, heads, together):
        group = range(first, first + together)
        cut = {h: [scores[h, :, pl.ds(0, ahead)], scores[h, :, pl.ds(ahead, v_own.shape[0])]] for h in group}
        held = {h: [v_st[pl.ds(0, ahead), columns[h]], v_own[:, columns[h]]] for h in group}
        if late:
            for h in group:
                cut[h].append(scored(q_all[:, columns[h]], k_new[:, columns[h]]))
                held[h].append(v_new[:, columns[h]])
        peaks = {h: row_fold(jnp.maximum, jnp.max, cut[h]) for h in group}
        powered, summed = {}, {}
        for h in group:
            powered[h] = [jnp.exp2(part - peaks[h]) for part in cut[h]]
            summed[h] = jnp.dot(
                jnp.concatenate([part.astype(jnp.bfloat16) for part in powered[h]], axis=1),
                jnp.concatenate(held[h], axis=0),
                preferred_element_type=jnp.float32,
            )
        totals = {h: row_fold(jnp.add, jnp.sum, powered[h]) for h in group}
        for h in group:
            result = (summed[h] / totals[h]).astype(jnp.bfloat16)
            for step in range(count):
                outs[step][:, columns[h]] = result[step * rows : (step + 1) * rows]


def row_fold(both, along, parts):
    blocks = [part[:, at : at + 128] for part in parts for at in range(0, part.shape[1], 128)]
    return along(functools.reduce(both, blocks), axis=-1, keepdims=True)


def join_kernel(count, me, *refs):
    parts, out = in_turn(refs[:count], tokens_out), refs[count]
    width = parts[0].shape[1]
    for step in range(count):
        out[:, pl.ds(pl.multiple_of((me[0] ^ step) * width, 128), width)] = parts[step][...]


def local(
    head_n,
    patch_n,
    queries,
    keys,
    values,
    q_gain,
    k_gain,
    prev_keys,
    prev_values,
    res_keys,
    res_values,
    block_ids,
    scale_exps,
):
    bf16 = jnp.bfloat16
    heads = scale_exps.shape[1]
    width = prev_keys.shape[1]
    size = width // heads
    sent, block_len = res_keys.shape[:2]
    rows = queries.shape[0]
    tok = rows * head_n
    fresh = sent * block_len
    my_head = lax.axis_index("head").reshape(1)
    my_patch = lax.axis_index("patch").reshape(1)
    four = patch_n == 4
    grant = pltpu.CompilerParams(vmem_limit_bytes=8 * 2**20)
    larger = grant if four else pltpu.CompilerParams(vmem_limit_bytes=24 * 2**20)

    def shape(*dims):
        return jax.ShapeDtypeStruct(dims, bf16)

    inputs = (block_ids, scale_exps, res_keys, res_values, queries, q_gain, keys, k_gain, values)
    both, *parts = pl.pallas_call(
        functools.partial(prepare_kernel, head_n, len(inputs)),
        out_shape=[shape(2 * heads * fresh + tail, size)] + [shape(3 * rows, width)] * head_n,
        in_specs=[SM] + [HB] * len(inputs),
        out_specs=[VM] * (head_n + 1),
        scratch_shapes=[pltpu.SMEM(x.shape, x.dtype) for x in inputs[:2]]
        + [pltpu.VMEM(x.shape, x.dtype) for x in inputs[2:]]
        + [pltpu.SemaphoreType.DMA((len(inputs),))],
        compiler_params=grant,
        name="prepare",
    )(my_head, *[in_hbm(x) for x in inputs])

    if four:
        near = trade(both, "patch", 1, patch_n)
        far = trade(both, "patch", 2, patch_n)
        residuals = [far]
        steps, late = [2, 1, 3], [near]
    else:
        residuals = [lax.all_gather(both, "patch", axis=0)]
        steps, late = range(1, patch_n), []
    parts = [trade(parts[step], "head", step, head_n) if step else parts[0] for step in range(head_n)]
    now = late
    late = [trade(far, "patch", 1, patch_n)] if four else []

    others = (patch_n - 1) * tok
    stale_k, stale_v = pl.pallas_call(
        functools.partial(stage_kernel, steps, 1 if four else 0, tok, fresh, block_len, len(residuals)),
        out_shape=[shape(others, width)] * 2,
        in_specs=[SM] + [HB] * 2 + [VM] * len(residuals),
        out_specs=[VM] * 2,
        scratch_shapes=[pltpu.SemaphoreType.DMA((2 * (patch_n - 1),))],
        compiler_params=larger,
        name="stage",
    )(my_patch, in_hbm(prev_keys), in_hbm(prev_values), *residuals)

    ahead = others - (len(now) + len(late)) * tok
    own = (1 + len(now)) * tok
    kept = jax.ShapeDtypeStruct((heads, tok, ahead + own), jnp.float32)
    q_all, v_own, scores = pl.pallas_call(
        functools.partial(score_kernel, head_n, len(now), ahead, block_len, fresh, size),
        out_shape=[shape(tok, width), shape(own, width), kept],
        in_specs=[VM] * (head_n + 2 + len(now)),
        out_specs=[VM] * 3,
        scratch_shapes=[pltpu.VMEM((own, width), bf16)],
        compiler_params=larger,
        name="score",
    )(stale_k, stale_v, *now, *[parts[step] for step in tokens_in(head_n)])
    outs = pl.pallas_call(
        functools.partial(finish_kernel, head_n, len(late), ahead, block_len, fresh, size),
        out_shape=[shape(rows, width)] * head_n,
        in_specs=[VM] * (5 + len(late)),
        out_specs=[VM] * head_n,
        scratch_shapes=[pltpu.VMEM((tok, width), bf16)] * 2,
        compiler_params=larger,
        name="finish",
    )(stale_k, stale_v, q_all, v_own, scores, *late)
    outs = [trade(outs[step], "head", step, head_n) if step else outs[0] for step in range(head_n)]
    return pl.pallas_call(
        functools.partial(join_kernel, head_n),
        out_shape=shape(rows, width * head_n),
        in_specs=[SM] + [VM] * head_n,
        out_specs=VM,
        compiler_params=grant,
        name="join",
    )(my_head, *[outs[step] for step in tokens_out(head_n)])


def solution(mesh):
    in_specs = (
        P(("groups", "patch", "head"), None),
        P(("groups", "patch", "head"), None),
        P(("groups", "patch", "head"), None),
        P(),
        P(),
        P("groups", "head"),
        P("groups", "head"),
        P(("groups", "patch"), None, "head"),
        P(("groups", "patch"), None, "head"),
        P(("groups", "patch")),
        P(("groups", "patch"), "head"),
    )
    out_specs = P(("groups", "patch", "head"), None)
    body = functools.partial(local, mesh.shape["head"], mesh.shape["patch"])
    return jax.shard_map(body, mesh=mesh, in_specs=in_specs, out_specs=out_specs, check_vma=False)
```

```python
import functools
import math

import jax
import jax.numpy as jnp
from jax import lax
from jax.experimental import pallas as pl
from jax.experimental.pallas import tpu as pltpu
from jax.sharding import PartitionSpec as P

epsilon = 1e-06
tail = 16
VM = pl.BlockSpec(memory_space=pltpu.VMEM)
SM = pl.BlockSpec(memory_space=pltpu.SMEM)
HB = pl.BlockSpec(memory_space=pltpu.HBM)
in_hbm = functools.partial(pltpu.with_memory_space_constraint, memory_space=pltpu.HBM)


def trade(array, axis, step, count):
    return lax.ppermute(array, axis, [(i, i ^ step) for i in range(count)])


def tokens_in(count):
    return [*range(2, count), *range(min(2, count))]


def tokens_out(count):
    return list(reversed(range(count)))


def in_turn(refs, order):
    turned = dict(zip(order(len(refs)), refs, strict=True))
    return [turned[step] for step in range(len(refs))]


def start_all(pairs, sems):
    copies = [pltpu.make_async_copy(a, b, sems.at[i]) for i, (a, b) in enumerate(pairs)]
    for copy in copies:
        copy.start()
    return copies


def prepare_kernel(count, n_in, me, *refs):
    inputs, both, outs = refs[:n_in], refs[n_in], refs[n_in + 1 : n_in + 1 + count]
    held, sems = refs[n_in + 1 + count : -1], refs[-1]
    copies = []
    for at, (source, target) in enumerate(zip(inputs, held, strict=True)):
        whole = pltpu.make_async_copy(source, target, sems.at[at])
        copies.append(whole)
        if at < 4 or len(source.shape) == 1 or source.shape[0] % 32:
            whole.start()
            continue
        high, wide = source.shape[0] // 2, source.shape[1] // 2
        for top in (0, high):
            for left in (0, wide):
                where = (pl.ds(top, high), pl.ds(left, wide))
                pltpu.make_async_copy(source.at[where], target.at[where], sems.at[at]).start()
    ids, exps, res_k, res_v, q_ref, qg_ref, k_ref, kg_ref, v_ref = held

    sent, block_len = res_k.shape[:2]
    heads = exps.shape[1]
    size = res_k.shape[2] // heads
    after = heads * sent * block_len + tail
    for copy in copies[:4]:
        copy.wait()
    for h in range(heads):
        for r in range(sent):
            power = (1 << (exps[r, h] + 16)).astype(jnp.float32) * (1.0 / 65536.0)
            lanes = pl.ds(h * size, size)
            at = (h * sent + r) * block_len
            k = (res_k[r, :, lanes].astype(jnp.float32) * power).astype(jnp.bfloat16)
            v = (res_v[r, :, lanes].astype(jnp.float32) * power).astype(jnp.bfloat16)
            both[pl.ds(at, block_len), :] = k
            both[pl.ds(after + at, block_len), :] = v
    lane = lax.broadcasted_iota(jnp.int32, (tail, size), 1) // block_len
    numbers = jnp.zeros((tail, size), jnp.float32)
    for r in range(sent):
        numbers = jnp.where(lane == r, ids[r].astype(jnp.float32), numbers)
    both[pl.ds(after - tail, tail), :] = numbers.astype(jnp.bfloat16)

    rows, width = q_ref.shape[0], q_ref.shape[1] // count
    columns = [pl.ds(pl.multiple_of((me[0] ^ step) * width, 128), width) for step in range(count)]
    for at, (ref, gain) in enumerate(((q_ref, qg_ref), (k_ref, kg_ref))):
        copies[4 + 2 * at].wait()
        copies[5 + 2 * at].wait()
        x = ref[...].astype(jnp.float32)
        inverse = lax.rsqrt(jnp.mean(x * x, axis=-1, keepdims=True) + epsilon)
        for step, cols in enumerate(columns):
            normal = ref[:, cols].astype(jnp.float32) * inverse * gain[cols]
            outs[step][pl.ds(at * rows, rows), :] = normal.astype(jnp.bfloat16)
    copies[8].wait()
    for step, cols in enumerate(columns):
        outs[step][pl.ds(2 * rows, rows), :] = v_ref[:, cols]


def chooser(tok, fresh, block_len, packed_k, rows_k):
    row = lax.broadcasted_iota(jnp.int32, (tok, fresh), 0)
    col = lax.broadcasted_iota(jnp.int32, (tok, fresh), 1)
    numbers = packed_k[pl.ds(rows_k, tail), :].astype(jnp.float32)[0:1, :fresh]
    return jnp.logical_and(
        row % block_len == col % block_len, (row // block_len).astype(jnp.float32) == numbers
    ).astype(jnp.bfloat16)


def refresh(chosen, old, source, new, target, residual, first):
    fresh = chosen.shape[1]
    size = residual.shape[1]
    for h in range(new.shape[1] // size):
        lanes = pl.ds(h * size, size)
        change = jnp.dot(
            chosen, residual[pl.ds(first + h * fresh, fresh), :], preferred_element_type=jnp.float32
        )
        new[target, lanes] = (old[source, lanes].astype(jnp.float32) + change).astype(jnp.bfloat16)


def stage_kernel(steps, early, tok, fresh, block_len, n_res, me, k_ref, v_ref, *refs):
    res, (k_out, v_out, sems) = refs[:n_res], refs[n_res:]
    pairs = []
    for place, step in enumerate(steps):
        source = pl.ds(pl.multiple_of((me[0] ^ step) * tok, 128), tok)
        target = pl.ds(place * tok, tok)
        pairs += [(k_ref.at[source], k_out.at[target]), (v_ref.at[source], v_out.at[target])]
    copies = start_all(pairs, sems)
    rows_k = k_out.shape[1] // res[0].shape[-1] * fresh

    def one(place, packed):
        rows = place * tok
        rows = pl.ds(rows if isinstance(place, int) else pl.multiple_of(rows, 128), tok)
        chosen = chooser(tok, fresh, block_len, packed, rows_k)
        refresh(chosen, k_out, rows, k_out, rows, packed, 0)
        refresh(chosen, v_out, rows, v_out, rows, packed, rows_k + tail)

    for copy in copies:
        copy.wait()
    if early:
        for place in range(early):
            one(place, res[place])
    else:

        @pl.loop(1, len(steps) + 1)
        def _(step):
            one(step - 1, res[0].at[me[0] ^ step])


def scored(q, keys):
    return lax.dot_general(
        q, keys, (((1,), (1,)), ((), ())), preferred_element_type=jnp.float32
    ) * (math.log2(math.e) / math.sqrt(q.shape[1]))


def score_kernel(count, n_now, ahead, block_len, fresh, size, *refs):
    (k_st, v_st), now, parts = refs[:2], refs[2 : 2 + n_now], in_turn(refs[2 + n_now : 2 + n_now + count], tokens_in)
    q_all, v_own, scores, k_own = refs[2 + n_now + count :]
    rows = parts[0].shape[0] // 3
    tok = rows * count
    heads = parts[0].shape[1] // size
    for place, packed in enumerate(now):
        chosen = chooser(tok, fresh, block_len, packed, heads * fresh)
        source, target = pl.ds(ahead + place * tok, tok), pl.ds((1 + place) * tok, tok)
        refresh(chosen, k_st, source, k_own, target, packed, 0)
        refresh(chosen, v_st, source, v_own, target, packed, heads * fresh + tail)
    for step in range(count):
        q_all[pl.ds(step * rows, rows), :] = parts[step][pl.ds(0, rows), :]
        k_own[pl.ds(step * rows, rows), :] = parts[step][pl.ds(rows, rows), :]
        v_own[pl.ds(step * rows, rows), :] = parts[step][pl.ds(2 * rows, rows), :]
    for h in range(heads):
        lanes = pl.ds(h * size, size)
        scores[h, :, pl.ds(0, ahead)] = scored(q_all[:, lanes], k_st[pl.ds(0, ahead), lanes])
        scores[h, :, pl.ds(ahead, k_own.shape[0])] = scored(q_all[:, lanes], k_own[:, lanes])


def finish_kernel(steps, n_late, n_given, rows, ahead, block_len, fresh, size, *refs):
    (k_st, v_st, q_all, v_own, scores), late = refs[:5], refs[5 : 5 + n_late]
    given = refs[5 + n_late : 5 + n_late + n_given]
    outs = refs[5 + n_late + n_given :]
    tok = q_all.shape[0]
    heads = q_all.shape[1] // size
    k_new, v_new = given or outs[len(steps) :] or (None, None)
    for packed in late:
        chosen = chooser(tok, fresh, block_len, packed, heads * fresh)
        source, target = pl.ds(k_st.shape[0] - tok, tok), pl.ds(0, tok)
        refresh(chosen, k_st, source, k_new, target, packed, 0)
        refresh(chosen, v_st, source, v_new, target, packed, heads * fresh + tail)
    span = pl.ds(steps[0] * rows, len(steps) * rows)
    columns = [pl.ds(h * size, size) for h in range(heads)]
    together = heads if k_new is not None else 1
    for first in range(0, heads, together):
        group = range(first, first + together)
        cut = {h: [scores[h, span, pl.ds(0, ahead)], scores[h, span, pl.ds(ahead, v_own.shape[0])]] for h in group}
        held = {h: [v_st[pl.ds(0, ahead), columns[h]], v_own[:, columns[h]]] for h in group}
        if k_new is not None:
            for h in group:
                cut[h].append(scored(q_all[span, columns[h]], k_new[:, columns[h]]))
                held[h].append(v_new[:, columns[h]])
        peaks = {h: row_fold(jnp.maximum, jnp.max, cut[h]) for h in group}
        powered, summed = {}, {}
        for h in group:
            powered[h] = [jnp.exp2(part - peaks[h]) for part in cut[h]]
            summed[h] = jnp.dot(
                jnp.concatenate([part.astype(jnp.bfloat16) for part in powered[h]], axis=1),
                jnp.concatenate(held[h], axis=0),
                preferred_element_type=jnp.float32,
            )
        totals = {h: row_fold(jnp.add, jnp.sum, powered[h]) for h in group}
        for h in group:
            result = (summed[h] / totals[h]).astype(jnp.bfloat16)
            for place in range(len(steps)):
                outs[place][:, columns[h]] = result[place * rows : (place + 1) * rows]


def row_fold(both, along, parts):
    blocks = [part[:, at : at + 128] for part in parts for at in range(0, part.shape[1], 128)]
    return along(functools.reduce(both, blocks), axis=-1, keepdims=True)


def join_kernel(count, me, *refs):
    parts, out = in_turn(refs[:count], tokens_out), refs[count]
    width = parts[0].shape[1]
    for step in range(count):
        out[:, pl.ds(pl.multiple_of((me[0] ^ step) * width, 128), width)] = parts[step][...]


def local(
    head_n,
    patch_n,
    queries,
    keys,
    values,
    q_gain,
    k_gain,
    prev_keys,
    prev_values,
    res_keys,
    res_values,
    block_ids,
    scale_exps,
):
    bf16 = jnp.bfloat16
    heads = scale_exps.shape[1]
    width = prev_keys.shape[1]
    size = width // heads
    sent, block_len = res_keys.shape[:2]
    rows = queries.shape[0]
    tok = rows * head_n
    fresh = sent * block_len
    my_head = lax.axis_index("head").reshape(1)
    my_patch = lax.axis_index("patch").reshape(1)
    four = patch_n == 4
    grant = pltpu.CompilerParams(vmem_limit_bytes=8 * 2**20)
    larger = grant if four else pltpu.CompilerParams(vmem_limit_bytes=24 * 2**20)

    def shape(*dims):
        return jax.ShapeDtypeStruct(dims, bf16)

    inputs = (block_ids, scale_exps, res_keys, res_values, queries, q_gain, keys, k_gain, values)
    both, *parts = pl.pallas_call(
        functools.partial(prepare_kernel, head_n, len(inputs)),
        out_shape=[shape(2 * heads * fresh + tail, size)] + [shape(3 * rows, width)] * head_n,
        in_specs=[SM] + [HB] * len(inputs),
        out_specs=[VM] * (head_n + 1),
        scratch_shapes=[pltpu.SMEM(x.shape, x.dtype) for x in inputs[:2]]
        + [pltpu.VMEM(x.shape, x.dtype) for x in inputs[2:]]
        + [pltpu.SemaphoreType.DMA((len(inputs),))],
        compiler_params=grant,
        name="prepare",
    )(my_head, *[in_hbm(x) for x in inputs])

    if four:
        near = trade(both, "patch", 1, patch_n)
        far = trade(both, "patch", 2, patch_n)
        residuals = [far]
        steps, late = [2, 1, 3], [near]
    else:
        residuals = [lax.all_gather(both, "patch", axis=0)]
        steps, late = range(1, patch_n), []
    parts = [trade(parts[step], "head", step, head_n) if step else parts[0] for step in range(head_n)]
    now = late
    late = [trade(far, "patch", 1, patch_n)] if four else []

    others = (patch_n - 1) * tok
    stale_k, stale_v = pl.pallas_call(
        functools.partial(stage_kernel, steps, 1 if four else 0, tok, fresh, block_len, len(residuals)),
        out_shape=[shape(others, width)] * 2,
        in_specs=[SM] + [HB] * 2 + [VM] * len(residuals),
        out_specs=[VM] * 2,
        scratch_shapes=[pltpu.SemaphoreType.DMA((2 * (patch_n - 1),))],
        compiler_params=larger,
        name="stage",
    )(my_patch, in_hbm(prev_keys), in_hbm(prev_values), *residuals)

    ahead = others - (len(now) + len(late)) * tok
    own = (1 + len(now)) * tok
    kept = jax.ShapeDtypeStruct((heads, tok, ahead + own), jnp.float32)
    q_all, v_own, scores = pl.pallas_call(
        functools.partial(score_kernel, head_n, len(now), ahead, block_len, fresh, size),
        out_shape=[shape(tok, width), shape(own, width), kept],
        in_specs=[VM] * (head_n + 2 + len(now)),
        out_specs=[VM] * 3,
        scratch_shapes=[pltpu.VMEM((own, width), bf16)],
        compiler_params=larger,
        name="score",
    )(stale_k, stale_v, *now, *[parts[step] for step in tokens_in(head_n)])
    done, given = {}, []
    for steps in (range(2, head_n), range(min(2, head_n))):
        fresh_late = [] if given else late
        finished = pl.pallas_call(
            functools.partial(finish_kernel, steps, len(fresh_late), len(given), rows, ahead, block_len, fresh, size),
            out_shape=[shape(rows, width)] * len(steps) + [shape(tok, width)] * (2 * len(fresh_late)),
            in_specs=[VM] * (5 + len(fresh_late) + len(given)),
            out_specs=[VM] * (len(steps) + 2 * len(fresh_late)),
            compiler_params=larger,
            name="finish",
        )(stale_k, stale_v, q_all, v_own, scores, *fresh_late, *given)
        done.update(zip(steps, finished))
        given = given or finished[len(steps) :]
    outs = [done[step] for step in range(head_n)]
    outs = [trade(outs[step], "head", step, head_n) if step else outs[0] for step in range(head_n)]
    return pl.pallas_call(
        functools.partial(join_kernel, head_n),
        out_shape=shape(rows, width * head_n),
        in_specs=[SM] + [VM] * head_n,
        out_specs=VM,
        compiler_params=grant,
        name="join",
    )(my_head, *[outs[step] for step in tokens_out(head_n)])


def solution(mesh):
    in_specs = (
        P(("groups", "patch", "head"), None),
        P(("groups", "patch", "head"), None),
        P(("groups", "patch", "head"), None),
        P(),
        P(),
        P("groups", "head"),
        P("groups", "head"),
        P(("groups", "patch"), None, "head"),
        P(("groups", "patch"), None, "head"),
        P(("groups", "patch")),
        P(("groups", "patch"), "head"),
    )
    out_specs = P(("groups", "patch", "head"), None)
    body = functools.partial(local, mesh.shape["head"], mesh.shape["patch"])
    return jax.shard_map(body, mesh=mesh, in_specs=in_specs, out_specs=out_specs, check_vma=False)
```

```python
import functools
import math

import jax
import jax.numpy as jnp
from jax import lax
from jax.experimental import pallas as pl
from jax.experimental.pallas import tpu as pltpu
from jax.sharding import PartitionSpec as P

epsilon = 1e-06
tail = 16
VM = pl.BlockSpec(memory_space=pltpu.VMEM)
SM = pl.BlockSpec(memory_space=pltpu.SMEM)
HB = pl.BlockSpec(memory_space=pltpu.HBM)
in_hbm = functools.partial(pltpu.with_memory_space_constraint, memory_space=pltpu.HBM)


def trade(array, axis, step, count):
    return lax.ppermute(array, axis, [(i, i ^ step) for i in range(count)])


def tokens_in(count):
    return [*range(2, count), *range(min(2, count))]


def tokens_out(count):
    return list(reversed(range(count)))


def in_turn(refs, order):
    turned = dict(zip(order(len(refs)), refs, strict=True))
    return [turned[step] for step in range(len(refs))]


def start_all(pairs, sems):
    copies = [pltpu.make_async_copy(a, b, sems.at[i]) for i, (a, b) in enumerate(pairs)]
    for copy in copies:
        copy.start()
    return copies


def prepare_kernel(count, n_in, me, *refs):
    inputs, both, outs = refs[:n_in], refs[n_in], refs[n_in + 1 : n_in + 1 + count]
    held, sems = refs[n_in + 1 + count : -1], refs[-1]
    copies = []
    for at, (source, target) in enumerate(zip(inputs, held, strict=True)):
        whole = pltpu.make_async_copy(source, target, sems.at[at])
        copies.append(whole)
        if at < 4 or len(source.shape) == 1 or source.shape[0] % 32:
            whole.start()
            continue
        high, wide = source.shape[0] // 2, source.shape[1] // 2
        for top in (0, high):
            for left in (0, wide):
                where = (pl.ds(top, high), pl.ds(left, wide))
                pltpu.make_async_copy(source.at[where], target.at[where], sems.at[at]).start()
    ids, exps, res_k, res_v, q_ref, qg_ref, k_ref, kg_ref, v_ref = held

    sent, block_len = res_k.shape[:2]
    heads = exps.shape[1]
    size = res_k.shape[2] // heads
    after = heads * sent * block_len + tail
    for copy in copies[:4]:
        copy.wait()
    for h in range(heads):
        for r in range(sent):
            power = (1 << (exps[r, h] + 16)).astype(jnp.float32) * (1.0 / 65536.0)
            lanes = pl.ds(h * size, size)
            at = (h * sent + r) * block_len
            k = (res_k[r, :, lanes].astype(jnp.float32) * power).astype(jnp.bfloat16)
            v = (res_v[r, :, lanes].astype(jnp.float32) * power).astype(jnp.bfloat16)
            both[pl.ds(at, block_len), :] = k
            both[pl.ds(after + at, block_len), :] = v
    lane = lax.broadcasted_iota(jnp.int32, (tail, size), 1) // block_len
    numbers = jnp.zeros((tail, size), jnp.float32)
    for r in range(sent):
        numbers = jnp.where(lane == r, ids[r].astype(jnp.float32), numbers)
    both[pl.ds(after - tail, tail), :] = numbers.astype(jnp.bfloat16)

    rows, width = q_ref.shape[0], q_ref.shape[1] // count
    columns = [pl.ds(pl.multiple_of((me[0] ^ step) * width, 128), width) for step in range(count)]
    for at, (ref, gain) in enumerate(((q_ref, qg_ref), (k_ref, kg_ref))):
        copies[4 + 2 * at].wait()
        copies[5 + 2 * at].wait()
        x = ref[...].astype(jnp.float32)
        inverse = lax.rsqrt(jnp.mean(x * x, axis=-1, keepdims=True) + epsilon)
        for step, cols in enumerate(columns):
            normal = ref[:, cols].astype(jnp.float32) * inverse * gain[cols]
            outs[step][pl.ds(at * rows, rows), :] = normal.astype(jnp.bfloat16)
    copies[8].wait()
    for step, cols in enumerate(columns):
        outs[step][pl.ds(2 * rows, rows), :] = v_ref[:, cols]


def chooser(tok, fresh, block_len, packed_k, rows_k):
    row = lax.broadcasted_iota(jnp.int32, (tok, fresh), 0)
    col = lax.broadcasted_iota(jnp.int32, (tok, fresh), 1)
    numbers = packed_k[pl.ds(rows_k, tail), :].astype(jnp.float32)[0:1, :fresh]
    return jnp.logical_and(
        row % block_len == col % block_len, (row // block_len).astype(jnp.float32) == numbers
    ).astype(jnp.bfloat16)


def refresh(chosen, old, source, new, target, residual, first):
    fresh = chosen.shape[1]
    size = residual.shape[1]
    for h in range(new.shape[1] // size):
        lanes = pl.ds(h * size, size)
        change = jnp.dot(
            chosen, residual[pl.ds(first + h * fresh, fresh), :], preferred_element_type=jnp.float32
        )
        new[target, lanes] = (old[source, lanes].astype(jnp.float32) + change).astype(jnp.bfloat16)


def stage_kernel(steps, early, tok, fresh, block_len, n_res, me, k_ref, v_ref, *refs):
    res, (k_out, v_out, sems) = refs[:n_res], refs[n_res:]
    pairs = []
    for place, step in enumerate(steps):
        source = pl.ds(pl.multiple_of((me[0] ^ step) * tok, 128), tok)
        target = pl.ds(place * tok, tok)
        pairs += [(k_ref.at[source], k_out.at[target]), (v_ref.at[source], v_out.at[target])]
    copies = start_all(pairs, sems)
    rows_k = k_out.shape[1] // res[0].shape[-1] * fresh

    def one(place, packed):
        rows = place * tok
        rows = pl.ds(rows if isinstance(place, int) else pl.multiple_of(rows, 128), tok)
        chosen = chooser(tok, fresh, block_len, packed, rows_k)
        refresh(chosen, k_out, rows, k_out, rows, packed, 0)
        refresh(chosen, v_out, rows, v_out, rows, packed, rows_k + tail)

    for copy in copies:
        copy.wait()
    if early:
        for place in range(early):
            one(place, res[place])
    else:

        @pl.loop(1, len(steps) + 1)
        def _(step):
            one(step - 1, res[0].at[me[0] ^ step])


def scored(q, keys):
    return lax.dot_general(
        q, keys, (((1,), (1,)), ((), ())), preferred_element_type=jnp.float32
    ) * (math.log2(math.e) / math.sqrt(q.shape[1]))


def near_kernel(tok, block_len, fresh, size, k_st, v_st, packed, *refs):
    k_out, v_out = refs[-2:]
    rows_k = k_st.shape[1] // size * fresh
    chosen = chooser(tok, fresh, block_len, packed, rows_k)
    refresh(chosen, k_st, pl.ds(tok, tok), k_out, pl.ds(0, tok), packed, 0)
    refresh(chosen, v_st, pl.ds(tok, tok), v_out, pl.ds(0, tok), packed, rows_k + tail)


def score_kernel(count, n_now, ahead, block_len, fresh, size, *refs):
    (k_st, v_st), now, parts = refs[:2], refs[2 : 2 + n_now], in_turn(refs[2 + n_now : 2 + n_now + count], tokens_in)
    q_all, v_own, scores, k_own = refs[2 + n_now + count :]
    near = pl.ds(parts[0].shape[0] // 3 * count, parts[0].shape[0] // 3 * count)
    rows = parts[0].shape[0] // 3
    tok = rows * count
    heads = parts[0].shape[1] // size
    if now:
        k_own[near, :] = now[0][...]
        v_own[near, :] = now[1][...]
    for step in range(count):
        q_all[pl.ds(step * rows, rows), :] = parts[step][pl.ds(0, rows), :]
        k_own[pl.ds(step * rows, rows), :] = parts[step][pl.ds(rows, rows), :]
        v_own[pl.ds(step * rows, rows), :] = parts[step][pl.ds(2 * rows, rows), :]
    for h in range(heads):
        lanes = pl.ds(h * size, size)
        scores[h, :, pl.ds(0, ahead)] = scored(q_all[:, lanes], k_st[pl.ds(0, ahead), lanes])
        scores[h, :, pl.ds(ahead, k_own.shape[0])] = scored(q_all[:, lanes], k_own[:, lanes])


def finish_kernel(steps, n_late, n_given, rows, ahead, block_len, fresh, size, *refs):
    (k_st, v_st, q_all, v_own, scores), late = refs[:5], refs[5 : 5 + n_late]
    given = refs[5 + n_late : 5 + n_late + n_given]
    outs = refs[5 + n_late + n_given :]
    tok = q_all.shape[0]
    heads = q_all.shape[1] // size
    k_new, v_new = given or outs[len(steps) :] or (None, None)
    for packed in late:
        chosen = chooser(tok, fresh, block_len, packed, heads * fresh)
        source, target = pl.ds(k_st.shape[0] - tok, tok), pl.ds(0, tok)
        refresh(chosen, k_st, source, k_new, target, packed, 0)
        refresh(chosen, v_st, source, v_new, target, packed, heads * fresh + tail)
    span = pl.ds(steps[0] * rows, len(steps) * rows)
    columns = [pl.ds(h * size, size) for h in range(heads)]
    together = heads if k_new is not None else 1
    for first in range(0, heads, together):
        group = range(first, first + together)
        cut = {h: [scores[h, span, pl.ds(0, ahead)], scores[h, span, pl.ds(ahead, v_own.shape[0])]] for h in group}
        held = {h: [v_st[pl.ds(0, ahead), columns[h]], v_own[:, columns[h]]] for h in group}
        if k_new is not None:
            for h in group:
                cut[h].append(scored(q_all[span, columns[h]], k_new[:, columns[h]]))
                held[h].append(v_new[:, columns[h]])
        peaks = {h: row_fold(jnp.maximum, jnp.max, cut[h]) for h in group}
        powered, summed = {}, {}
        for h in group:
            powered[h] = [jnp.exp2(part - peaks[h]) for part in cut[h]]
            summed[h] = jnp.dot(
                jnp.concatenate([part.astype(jnp.bfloat16) for part in powered[h]], axis=1),
                jnp.concatenate(held[h], axis=0),
                preferred_element_type=jnp.float32,
            )
        totals = {h: row_fold(jnp.add, jnp.sum, powered[h]) for h in group}
        for h in group:
            result = (summed[h] / totals[h]).astype(jnp.bfloat16)
            for place in range(len(steps)):
                outs[place][:, columns[h]] = result[place * rows : (place + 1) * rows]


def row_fold(both, along, parts):
    blocks = [part[:, at : at + 128] for part in parts for at in range(0, part.shape[1], 128)]
    return along(functools.reduce(both, blocks), axis=-1, keepdims=True)


def join_kernel(count, me, *refs):
    parts, out = in_turn(refs[:count], tokens_out), refs[count]
    width = parts[0].shape[1]
    for step in range(count):
        out[:, pl.ds(pl.multiple_of((me[0] ^ step) * width, 128), width)] = parts[step][...]


def local(
    head_n,
    patch_n,
    queries,
    keys,
    values,
    q_gain,
    k_gain,
    prev_keys,
    prev_values,
    res_keys,
    res_values,
    block_ids,
    scale_exps,
):
    bf16 = jnp.bfloat16
    heads = scale_exps.shape[1]
    width = prev_keys.shape[1]
    size = width // heads
    sent, block_len = res_keys.shape[:2]
    rows = queries.shape[0]
    tok = rows * head_n
    fresh = sent * block_len
    my_head = lax.axis_index("head").reshape(1)
    my_patch = lax.axis_index("patch").reshape(1)
    four = patch_n == 4
    grant = pltpu.CompilerParams(vmem_limit_bytes=8 * 2**20)
    larger = grant if four else pltpu.CompilerParams(vmem_limit_bytes=24 * 2**20)

    def shape(*dims):
        return jax.ShapeDtypeStruct(dims, bf16)

    inputs = (block_ids, scale_exps, res_keys, res_values, queries, q_gain, keys, k_gain, values)
    both, *parts = pl.pallas_call(
        functools.partial(prepare_kernel, head_n, len(inputs)),
        out_shape=[shape(2 * heads * fresh + tail, size)] + [shape(3 * rows, width)] * head_n,
        in_specs=[SM] + [HB] * len(inputs),
        out_specs=[VM] * (head_n + 1),
        scratch_shapes=[pltpu.SMEM(x.shape, x.dtype) for x in inputs[:2]]
        + [pltpu.VMEM(x.shape, x.dtype) for x in inputs[2:]]
        + [pltpu.SemaphoreType.DMA((len(inputs),))],
        compiler_params=grant,
        name="prepare",
    )(my_head, *[in_hbm(x) for x in inputs])

    if four:
        near = trade(both, "patch", 1, patch_n)
        far = trade(both, "patch", 2, patch_n)
        residuals = [far]
        steps, late = [2, 1, 3], [near]
    else:
        residuals = [lax.all_gather(both, "patch", axis=0)]
        steps, late = range(1, patch_n), []
    parts = [trade(parts[step], "head", step, head_n) if step else parts[0] for step in range(head_n)]
    now = late
    late = [trade(far, "patch", 1, patch_n)] if four else []

    others = (patch_n - 1) * tok
    stale_k, stale_v = pl.pallas_call(
        functools.partial(stage_kernel, steps, 1 if four else 0, tok, fresh, block_len, len(residuals)),
        out_shape=[shape(others, width)] * 2,
        in_specs=[SM] + [HB] * 2 + [VM] * len(residuals),
        out_specs=[VM] * 2,
        scratch_shapes=[pltpu.SemaphoreType.DMA((2 * (patch_n - 1),))],
        compiler_params=larger,
        name="stage",
    )(my_patch, in_hbm(prev_keys), in_hbm(prev_values), *residuals)

    ahead = others - 2 * tok if four else others
    own = (2 if four else 1) * tok
    if now:
        now = pl.pallas_call(
            functools.partial(near_kernel, tok, block_len, fresh, size),
            out_shape=[shape(tok, width)] * 2,
            in_specs=[VM] * (1 + head_n),
            out_specs=[VM] * 2,
            compiler_params=grant,
            cost_estimate=pl.CostEstimate(flops=500000000, bytes_accessed=0, transcendentals=0),
            name="near",
        )(stale_k, stale_v, *now, *parts[2:])
    kept = jax.ShapeDtypeStruct((heads, tok, ahead + own), jnp.float32)
    q_all, v_own, scores = pl.pallas_call(
        functools.partial(score_kernel, head_n, len(now), ahead, block_len, fresh, size),
        out_shape=[shape(tok, width), shape(own, width), kept],
        in_specs=[VM] * (head_n + 2 + len(now)),
        out_specs=[VM] * 3,
        scratch_shapes=[pltpu.VMEM((own, width), bf16)],
        compiler_params=larger,
        name="score",
    )(stale_k, stale_v, *now, *[parts[step] for step in tokens_in(head_n)])
    done, given = {}, []
    for steps in (range(2, head_n), range(min(2, head_n))):
        fresh_late = [] if given else late
        finished = pl.pallas_call(
            functools.partial(finish_kernel, steps, len(fresh_late), len(given), rows, ahead, block_len, fresh, size),
            out_shape=[shape(rows, width)] * len(steps) + [shape(tok, width)] * (2 * len(fresh_late)),
            in_specs=[VM] * (5 + len(fresh_late) + len(given)),
            out_specs=[VM] * (len(steps) + 2 * len(fresh_late)),
            compiler_params=larger,
            name="finish",
        )(stale_k, stale_v, q_all, v_own, scores, *fresh_late, *given)
        done.update(zip(steps, finished))
        given = given or finished[len(steps) :]
    outs = [done[step] for step in range(head_n)]
    outs = [trade(outs[step], "head", step, head_n) if step else outs[0] for step in range(head_n)]
    return pl.pallas_call(
        functools.partial(join_kernel, head_n),
        out_shape=shape(rows, width * head_n),
        in_specs=[SM] + [VM] * head_n,
        out_specs=VM,
        compiler_params=grant,
        name="join",
    )(my_head, *[outs[step] for step in tokens_out(head_n)])


def solution(mesh):
    in_specs = (
        P(("groups", "patch", "head"), None),
        P(("groups", "patch", "head"), None),
        P(("groups", "patch", "head"), None),
        P(),
        P(),
        P("groups", "head"),
        P("groups", "head"),
        P(("groups", "patch"), None, "head"),
        P(("groups", "patch"), None, "head"),
        P(("groups", "patch")),
        P(("groups", "patch"), "head"),
    )
    out_specs = P(("groups", "patch", "head"), None)
    body = functools.partial(local, mesh.shape["head"], mesh.shape["patch"])
    return jax.shard_map(body, mesh=mesh, in_specs=in_specs, out_specs=out_specs, check_vma=False)
```

```python
import functools
import math

import jax
import jax.numpy as jnp
from jax import lax
from jax.experimental import pallas as pl
from jax.experimental.pallas import tpu as pltpu
from jax.sharding import PartitionSpec as P

epsilon = 1e-06
tail = 16
VM = pl.BlockSpec(memory_space=pltpu.VMEM)
SM = pl.BlockSpec(memory_space=pltpu.SMEM)
HB = pl.BlockSpec(memory_space=pltpu.HBM)
in_hbm = functools.partial(pltpu.with_memory_space_constraint, memory_space=pltpu.HBM)


def trade(array, axis, step, count):
    return lax.ppermute(array, axis, [(i, i ^ step) for i in range(count)])


def cross(array, even, odd, patch_n, head_n):
    pairs = [(p * head_n + h, (p ^ (odd if h % 2 else even)) * head_n + h) for p in range(patch_n) for h in range(head_n)]
    return lax.ppermute(array, ("patch", "head"), pairs)


def tokens_in(count):
    return [*range(2, count), *range(min(2, count))]


def tokens_out(count):
    return [*range(2, count), *range(min(2, count))]


def in_turn(refs, order):
    turned = dict(zip(order(len(refs)), refs, strict=True))
    return [turned[step] for step in range(len(refs))]


def start_all(pairs, sems):
    copies = [pltpu.make_async_copy(a, b, sems.at[i]) for i, (a, b) in enumerate(pairs)]
    for copy in copies:
        copy.start()
    return copies


def prepare_kernel(count, n_in, me, *refs):
    inputs, both, outs = refs[:n_in], refs[n_in], refs[n_in + 1 : n_in + 1 + count]
    held, sems = refs[n_in + 1 + count : -1], refs[-1]
    copies = []
    for at, (source, target) in enumerate(zip(inputs, held, strict=True)):
        whole = pltpu.make_async_copy(source, target, sems.at[at])
        copies.append(whole)
        if at < 4 or len(source.shape) == 1 or source.shape[0] % 32:
            whole.start()
            continue
        high, wide = source.shape[0] // 2, source.shape[1] // 2
        for top in (0, high):
            for left in (0, wide):
                where = (pl.ds(top, high), pl.ds(left, wide))
                pltpu.make_async_copy(source.at[where], target.at[where], sems.at[at]).start()
    ids, exps, res_k, res_v, q_ref, qg_ref, k_ref, kg_ref, v_ref = held

    sent, block_len = res_k.shape[:2]
    heads = exps.shape[1]
    size = res_k.shape[2] // heads
    after = heads * sent * block_len + tail
    for copy in copies[:4]:
        copy.wait()
    for h in range(heads):
        for r in range(sent):
            power = (1 << (exps[r, h] + 16)).astype(jnp.float32) * (1.0 / 65536.0)
            lanes = pl.ds(h * size, size)
            at = (h * sent + r) * block_len
            k = (res_k[r, :, lanes].astype(jnp.float32) * power).astype(jnp.bfloat16)
            v = (res_v[r, :, lanes].astype(jnp.float32) * power).astype(jnp.bfloat16)
            both[pl.ds(at, block_len), :] = k
            both[pl.ds(after + at, block_len), :] = v
    lane = lax.broadcasted_iota(jnp.int32, (tail, size), 1) // block_len
    numbers = jnp.zeros((tail, size), jnp.float32)
    for r in range(sent):
        numbers = jnp.where(lane == r, ids[r].astype(jnp.float32), numbers)
    both[pl.ds(after - tail, tail), :] = numbers.astype(jnp.bfloat16)

    rows, width = q_ref.shape[0], q_ref.shape[1] // count
    columns = [pl.ds(pl.multiple_of((me[0] ^ step) * width, 128), width) for step in range(count)]
    for at, (ref, gain) in enumerate(((q_ref, qg_ref), (k_ref, kg_ref))):
        copies[4 + 2 * at].wait()
        copies[5 + 2 * at].wait()
        x = ref[...].astype(jnp.float32)
        inverse = lax.rsqrt(jnp.mean(x * x, axis=-1, keepdims=True) + epsilon)
        for step, cols in enumerate(columns):
            normal = ref[:, cols].astype(jnp.float32) * inverse * gain[cols]
            outs[step][pl.ds(at * rows, rows), :] = normal.astype(jnp.bfloat16)
    copies[8].wait()
    for step, cols in enumerate(columns):
        outs[step][pl.ds(2 * rows, rows), :] = v_ref[:, cols]


def chooser(tok, fresh, block_len, packed_k, rows_k):
    row = lax.broadcasted_iota(jnp.int32, (tok, fresh), 0)
    col = lax.broadcasted_iota(jnp.int32, (tok, fresh), 1)
    numbers = packed_k[pl.ds(rows_k, tail), :].astype(jnp.float32)[0:1, :fresh]
    return jnp.logical_and(
        row % block_len == col % block_len, (row // block_len).astype(jnp.float32) == numbers
    ).astype(jnp.bfloat16)


def refresh(chosen, old, source, new, target, residual, first):
    fresh = chosen.shape[1]
    size = residual.shape[1]
    for h in range(new.shape[1] // size):
        lanes = pl.ds(h * size, size)
        change = jnp.dot(
            chosen, residual[pl.ds(first + h * fresh, fresh), :], preferred_element_type=jnp.float32
        )
        new[target, lanes] = (old[source, lanes].astype(jnp.float32) + change).astype(jnp.bfloat16)


def stage_kernel(steps, early, tok, fresh, block_len, n_res, me, my_head, k_ref, v_ref, *refs):
    res, (k_out, v_out, sems) = refs[:n_res], refs[n_res:]
    pairs = []
    if early:
        first = 2 - my_head[0] % 2
        steps = [first, 3 - first, 3]
    for place, step in enumerate(steps):
        source = pl.ds(pl.multiple_of((me[0] ^ step) * tok, 128), tok)
        target = pl.ds(place * tok, tok)
        pairs += [(k_ref.at[source], k_out.at[target]), (v_ref.at[source], v_out.at[target])]
    copies = start_all(pairs, sems)
    rows_k = k_out.shape[1] // res[0].shape[-1] * fresh

    def one(place, packed):
        rows = place * tok
        rows = pl.ds(rows if isinstance(place, int) else pl.multiple_of(rows, 128), tok)
        chosen = chooser(tok, fresh, block_len, packed, rows_k)
        refresh(chosen, k_out, rows, k_out, rows, packed, 0)
        refresh(chosen, v_out, rows, v_out, rows, packed, rows_k + tail)

    for copy in copies:
        copy.wait()
    if early:
        for place in range(early):
            one(place, res[place])
    else:

        @pl.loop(1, len(steps) + 1)
        def _(step):
            one(step - 1, res[0].at[me[0] ^ step])


def scored(q, keys):
    return lax.dot_general(
        q, keys, (((1,), (1,)), ((), ())), preferred_element_type=jnp.float32
    ) * (math.log2(math.e) / math.sqrt(q.shape[1]))


def near_kernel(tok, block_len, fresh, size, k_st, v_st, packed, *refs):
    k_out, v_out = refs[-2:]
    rows_k = k_st.shape[1] // size * fresh
    chosen = chooser(tok, fresh, block_len, packed, rows_k)
    refresh(chosen, k_st, pl.ds(tok, tok), k_out, pl.ds(0, tok), packed, 0)
    refresh(chosen, v_st, pl.ds(tok, tok), v_out, pl.ds(0, tok), packed, rows_k + tail)


def score_kernel(count, n_now, ahead, block_len, fresh, size, *refs):
    (k_st, v_st), now, parts = refs[:2], refs[2 : 2 + n_now], in_turn(refs[2 + n_now : 2 + n_now + count], tokens_in)
    q_all, v_own, scores, k_own = refs[2 + n_now + count :]
    near = pl.ds(parts[0].shape[0] // 3 * count, parts[0].shape[0] // 3 * count)
    rows = parts[0].shape[0] // 3
    tok = rows * count
    heads = parts[0].shape[1] // size
    if now:
        k_own[near, :] = now[0][...]
        v_own[near, :] = now[1][...]
    for step in range(count):
        q_all[pl.ds(step * rows, rows), :] = parts[step][pl.ds(0, rows), :]
        k_own[pl.ds(step * rows, rows), :] = parts[step][pl.ds(rows, rows), :]
        v_own[pl.ds(step * rows, rows), :] = parts[step][pl.ds(2 * rows, rows), :]
    for h in range(heads):
        lanes = pl.ds(h * size, size)
        scores[h, :, pl.ds(0, ahead)] = scored(q_all[:, lanes], k_st[pl.ds(0, ahead), lanes])
        scores[h, :, pl.ds(ahead, k_own.shape[0])] = scored(q_all[:, lanes], k_own[:, lanes])


def finish_kernel(steps, n_late, n_given, rows, ahead, block_len, fresh, size, *refs):
    (k_st, v_st, q_all, v_own, scores), late = refs[:5], refs[5 : 5 + n_late]
    given = refs[5 + n_late : 5 + n_late + n_given]
    outs = refs[5 + n_late + n_given :]
    tok = q_all.shape[0]
    heads = q_all.shape[1] // size
    k_new, v_new = given or outs[len(steps) :] or (None, None)
    for packed in late:
        chosen = chooser(tok, fresh, block_len, packed, heads * fresh)
        source, target = pl.ds(k_st.shape[0] - tok, tok), pl.ds(0, tok)
        refresh(chosen, k_st, source, k_new, target, packed, 0)
        refresh(chosen, v_st, source, v_new, target, packed, heads * fresh + tail)
    span = pl.ds(steps[0] * rows, len(steps) * rows)
    columns = [pl.ds(h * size, size) for h in range(heads)]
    together = heads if k_new is not None else 1
    for first in range(0, heads, together):
        group = range(first, first + together)
        cut = {h: [scores[h, span, pl.ds(0, ahead)], scores[h, span, pl.ds(ahead, v_own.shape[0])]] for h in group}
        held = {h: [v_st[pl.ds(0, ahead), columns[h]], v_own[:, columns[h]]] for h in group}
        if k_new is not None:
            for h in group:
                cut[h].append(scored(q_all[span, columns[h]], k_new[:, columns[h]]))
                held[h].append(v_new[:, columns[h]])
        peaks = {h: row_fold(jnp.maximum, jnp.max, cut[h]) for h in group}
        powered, summed = {}, {}
        for h in group:
            powered[h] = [jnp.exp2(part - peaks[h]) for part in cut[h]]
            summed[h] = jnp.dot(
                jnp.concatenate([part.astype(jnp.bfloat16) for part in powered[h]], axis=1),
                jnp.concatenate(held[h], axis=0),
                preferred_element_type=jnp.float32,
            )
        totals = {h: row_fold(jnp.add, jnp.sum, powered[h]) for h in group}
        for h in group:
            result = (summed[h] / totals[h]).astype(jnp.bfloat16)
            for place in range(len(steps)):
                outs[place][:, columns[h]] = result[place * rows : (place + 1) * rows]


def row_fold(both, along, parts):
    blocks = [part[:, at : at + 128] for part in parts for at in range(0, part.shape[1], 128)]
    return along(functools.reduce(both, blocks), axis=-1, keepdims=True)


def join_kernel(count, me, *refs):
    parts, out = in_turn(refs[:count], tokens_out), refs[count]
    width = parts[0].shape[1]
    for step in range(count):
        out[:, pl.ds(pl.multiple_of((me[0] ^ step) * width, 128), width)] = parts[step][...]


def local(
    head_n,
    patch_n,
    queries,
    keys,
    values,
    q_gain,
    k_gain,
    prev_keys,
    prev_values,
    res_keys,
    res_values,
    block_ids,
    scale_exps,
):
    bf16 = jnp.bfloat16
    heads = scale_exps.shape[1]
    width = prev_keys.shape[1]
    size = width // heads
    sent, block_len = res_keys.shape[:2]
    rows = queries.shape[0]
    tok = rows * head_n
    fresh = sent * block_len
    my_head = lax.axis_index("head").reshape(1)
    my_patch = lax.axis_index("patch").reshape(1)
    four = patch_n == 4
    grant = pltpu.CompilerParams(vmem_limit_bytes=8 * 2**20)
    larger = grant if four else pltpu.CompilerParams(vmem_limit_bytes=24 * 2**20)

    def shape(*dims):
        return jax.ShapeDtypeStruct(dims, bf16)

    inputs = (block_ids, scale_exps, res_keys, res_values, queries, q_gain, keys, k_gain, values)
    both, *parts = pl.pallas_call(
        functools.partial(prepare_kernel, head_n, len(inputs)),
        out_shape=[shape(2 * heads * fresh + tail, size)] + [shape(3 * rows, width)] * head_n,
        in_specs=[SM] + [HB] * len(inputs),
        out_specs=[VM] * (head_n + 1),
        scratch_shapes=[pltpu.SMEM(x.shape, x.dtype) for x in inputs[:2]]
        + [pltpu.VMEM(x.shape, x.dtype) for x in inputs[2:]]
        + [pltpu.SemaphoreType.DMA((len(inputs),))],
        compiler_params=grant,
        name="prepare",
    )(my_head, *[in_hbm(x) for x in inputs])

    if four:
        first = cross(both, 2, 1, patch_n, head_n)
        second = cross(both, 1, 2, patch_n, head_n)
        residuals = [first]
        steps, late = [0, 0, 0], [second]
    else:
        residuals = [lax.all_gather(both, "patch", axis=0)]
        steps, late = range(1, patch_n), []
    parts = [trade(parts[step], "head", step, head_n) if step else parts[0] for step in range(head_n)]
    now = late
    late = [cross(first, 1, 2, patch_n, head_n)] if four else []

    others = (patch_n - 1) * tok
    stale_k, stale_v = pl.pallas_call(
        functools.partial(stage_kernel, steps, 1 if four else 0, tok, fresh, block_len, len(residuals)),
        out_shape=[shape(others, width)] * 2,
        in_specs=[SM] * 2 + [HB] * 2 + [VM] * len(residuals),
        out_specs=[VM] * 2,
        scratch_shapes=[pltpu.SemaphoreType.DMA((2 * (patch_n - 1),))],
        compiler_params=larger,
        name="stage",
    )(my_patch, my_head, in_hbm(prev_keys), in_hbm(prev_values), *residuals)

    ahead = others - 2 * tok if four else others
    own = (2 if four else 1) * tok
    if now:
        now = pl.pallas_call(
            functools.partial(near_kernel, tok, block_len, fresh, size),
            out_shape=[shape(tok, width)] * 2,
            in_specs=[VM] * (1 + head_n),
            out_specs=[VM] * 2,
            compiler_params=grant,
            cost_estimate=pl.CostEstimate(flops=500000000, bytes_accessed=0, transcendentals=0),
            name="near",
        )(stale_k, stale_v, *now, *parts[2:])
    kept = jax.ShapeDtypeStruct((heads, tok, ahead + own), jnp.float32)
    q_all, v_own, scores = pl.pallas_call(
        functools.partial(score_kernel, head_n, len(now), ahead, block_len, fresh, size),
        out_shape=[shape(tok, width), shape(own, width), kept],
        in_specs=[VM] * (head_n + 2 + len(now)),
        out_specs=[VM] * 3,
        scratch_shapes=[pltpu.VMEM((own, width), bf16)],
        compiler_params=larger,
        name="score",
    )(stale_k, stale_v, *now, *[parts[step] for step in tokens_in(head_n)])
    done, given = {}, []
    for steps in (range(2, head_n), range(min(2, head_n))):
        fresh_late = [] if given else late
        finished = pl.pallas_call(
            functools.partial(finish_kernel, steps, len(fresh_late), len(given), rows, ahead, block_len, fresh, size),
            out_shape=[shape(rows, width)] * len(steps) + [shape(tok, width)] * (2 * len(fresh_late)),
            in_specs=[VM] * (5 + len(fresh_late) + len(given)),
            out_specs=[VM] * (len(steps) + 2 * len(fresh_late)),
            compiler_params=larger,
            name="finish",
        )(stale_k, stale_v, q_all, v_own, scores, *fresh_late, *given)
        done.update(zip(steps, finished))
        given = given or finished[len(steps) :]
    outs = [done[step] for step in range(head_n)]
    outs = [trade(outs[step], "head", step, head_n) if step else outs[0] for step in range(head_n)]
    return pl.pallas_call(
        functools.partial(join_kernel, head_n),
        out_shape=shape(rows, width * head_n),
        in_specs=[SM] + [VM] * head_n,
        out_specs=VM,
        compiler_params=grant,
        name="join",
    )(my_head, *[outs[step] for step in tokens_out(head_n)])


def solution(mesh):
    in_specs = (
        P(("groups", "patch", "head"), None),
        P(("groups", "patch", "head"), None),
        P(("groups", "patch", "head"), None),
        P(),
        P(),
        P("groups", "head"),
        P("groups", "head"),
        P(("groups", "patch"), None, "head"),
        P(("groups", "patch"), None, "head"),
        P(("groups", "patch")),
        P(("groups", "patch"), "head"),
    )
    out_specs = P(("groups", "patch", "head"), None)
    body = functools.partial(local, mesh.shape["head"], mesh.shape["patch"])
    return jax.shard_map(body, mesh=mesh, in_specs=in_specs, out_specs=out_specs, check_vma=False)
```
